256 devices in a mesh: grid: 16 (over z, y_lo), dom: 16 (over y_hi, x, core).
Axes of the slice: x: 4, y: 4 (y_hi: 2, y_lo: 2; y = y_hi * 2 + y_lo), z: 8, core: 2. Of those that a mesh axis runs over, the one named last changes fastest.
Arguments:
- initial: float32 [16, 512, 64, 128], P('grid', 'dom'), may hold values from -6 to 6
- diffusion: float32 [16, 5], P('grid'), may hold values from 0.02 to 0.09
- drift: float32 [16, 5], P('grid'), may hold values from -0.15 to 0.15
- levels: int32 [16, 3], P('grid'), may hold values from 1 to 3, as said below
- weights: int32 [16], P('grid'), may hold values from -1 to 2, as said below
Outputs:
- stepped: float32 [16, 512, 64, 128], P('grid', 'dom')
- combined: float32 [512, 8, 8, 8, 128], P('dom')
The draws below stay inside these ranges and needn't reach their ends.
Inputs may be any that keep to these rules, and one draw needn't show every extreme that they name: Each row holds three levels whose sum is 6; grid 0 has a level 1 and a level 3. `weights`: every coefficient is one of -1, 1, 2.
All inputs are finite; a program needn't handle non-finite values.
Results may differ from the reference program's by a relative error of at most 0.00013.
Values sent between devices are 32-bit elements; how exact they have to be, the bound alone decides.
No kernel may reach another device: no remote copies, remote signals or barrier semaphores. Data moves between devices by JAX's collectives and lax.ppermute only.
A program may use at most 128 MiB of HBM per device.

```python
import math
import jax
import jax.numpy as jnp
import numpy as np
from jax import lax

MLEVEL = 3
MSUM = 6
LEN4 = 128
STEPS = 4
LEN0 = 512
SUB = 64
MLEN = 8
GRIDS = 16


def draw_levels(key, part):
    key = jax.random.fold_in(key, 11)
    triples = []
    anchored = []
    for first_level in range(1, MLEVEL + 1):
        for second_level in range(1, MLEVEL + 1):
            for third_level in range(1, MLEVEL + 1):
                if first_level + second_level + third_level == MSUM:
                    triples.append([first_level, second_level, third_level])
                    if min(first_level, second_level, third_level) == 1 and max(first_level, second_level, third_level) == MLEVEL:
                        anchored.append([first_level, second_level, third_level])
    triple_table = jnp.array(triples, jnp.int32)
    anchor_table = jnp.array(anchored, jnp.int32)
    chosen = jax.random.randint(jax.random.fold_in(key, 1), (GRIDS,), 0, len(triples))
    level_rows = triple_table[chosen]
    anchor_pick = jax.random.randint(jax.random.fold_in(key, 2), (), 0, len(anchored))
    level_rows = level_rows.at[0].set(anchor_table[anchor_pick])
    return level_rows.astype(jnp.int32)


def draw_weights(key, part):
    key = jax.random.fold_in(key, 23)
    values_table = jnp.array([1, -1, 2], jnp.int32)
    picked = jax.random.randint(key, (GRIDS,), 0, 3)
    coefficients = values_table[picked]
    coefficients = coefficients.at[0].set(2)
    coefficients = coefficients.at[1].set(-1)
    return coefficients.astype(jnp.int32)


def steps_of(own_key, shape, shards, smallest, top_value):
    gain = 1.0
    for axis_at, blocks in shards:
        steps = jax.random.uniform(jax.random.fold_in(jax.random.fold_in(own_key, 6), axis_at), (blocks,), jnp.float32, smallest / len(shards), top_value / len(shards))
        gain = gain * jnp.repeat(jnp.exp(steps), shape[axis_at] // blocks).reshape((-1,) + (1,) * (len(shape) - 1 - axis_at))
    return gain


def gaussian(own_key, extent, scale, limit, split=(), kind=jnp.bfloat16):
    values = jax.random.normal(own_key, extent, jnp.float32) * scale
    if len(split) > 0:
        values = steps_of(own_key, extent, split, -0.22, 0.18) * values
    return jnp.clip(values, min=-limit, max=limit).astype(kind)


def setup_inputs(seed: int = 0) -> dict:
    splits = jax.random.split(jax.random.key(seed), 6)
    return {
        "initial": gaussian(splits[0], (GRIDS, LEN0, SUB, LEN4), 1.0, 6.0, ((0, 16), (1, 16)), jnp.float32),
        "diffusion": jnp.clip(jnp.exp(math.log(0.09) - 1.50407746 * jax.random.uniform(splits[1], (GRIDS, 5), jnp.float32) ** steps_of(splits[1], (GRIDS, 5), ((0, 16),), -0.2, 0.2)), 0.02, 0.09),
        "drift": jnp.clip(jax.random.uniform(splits[2], (GRIDS, 5), jnp.float32, -0.15, 0.15) * steps_of(splits[2], (GRIDS, 5), ((0, 16),), -0.4, 0.0), -0.15, 0.15),
        "levels": draw_levels(jax.random.fold_in(splits[5], 71), 0),
        "weights": draw_weights(jax.random.fold_in(splits[5], 71), 0),
    }


def nodal_matrix(length_dim):
    matrix = np.eye(length_dim)
    stride = length_dim // 2
    while stride >= 1:
        for position in range(stride, length_dim, 2 * stride):
            matrix[position] = matrix[position] + 0.5 * matrix[position - stride]
            if position + stride < length_dim:
                matrix[position] = matrix[position] + 0.5 * matrix[position + stride]
        stride = stride // 2
    return matrix


def along_dim(values, matrix, dimension):
    product = jnp.tensordot(jnp.asarray(matrix, jnp.float32), values, axes=((1,), (dimension,)), precision=lax.Precision.HIGHEST)
    return jnp.moveaxis(product, 0, dimension)


def mid_coords(level_row, point_count):
    places = jnp.arange(point_count, dtype=jnp.int32)
    lengths = jnp.left_shift(jnp.ones((3,), jnp.int32), level_row.astype(jnp.int32))
    offsets = [level_row[1] + level_row[2], level_row[2], jnp.zeros((), jnp.int32)]
    coords = [jnp.bitwise_and(jnp.right_shift(places, offsets[dimension].astype(jnp.int32)), lengths[dimension] - 1) for dimension in range(3)]
    return coords, lengths


def mid_operator(level_row, spread_rate, drift_rate, point_count):
    coords, lengths = mid_coords(level_row, point_count)
    matrix = jnp.zeros((point_count, point_count), jnp.float32)
    identity = jnp.eye(point_count, dtype=jnp.float32)
    for dimension in range(3):
        aligned = jnp.ones((point_count, point_count), bool)
        for other in range(3):
            if other != dimension:
                aligned = aligned & (coords[other][:, None] == coords[other][None, :])
        upper_hit = aligned & (coords[dimension][None, :] == coords[dimension][:, None] + 1)
        lower_hit = aligned & (coords[dimension][None, :] == coords[dimension][:, None] - 1)
        spread_now = spread_rate[dimension + 1]
        drift_now = drift_rate[dimension + 1]
        matrix = matrix + upper_hit.astype(jnp.float32) * (spread_now + 0.5 * drift_now) + lower_hit.astype(jnp.float32) * (spread_now - 0.5 * drift_now)
        matrix = matrix - 2.0 * spread_now * identity
    return matrix


def mid_surplus(level_row, point_count):
    coords, lengths = mid_coords(level_row, point_count)
    matrix = jnp.ones((point_count, point_count), jnp.float32)
    for dimension in range(3):
        row_place = coords[dimension][:, None]
        col_place = coords[dimension][None, :]
        stride = jnp.bitwise_and(row_place, -row_place)
        interior = row_place > 0
        factor = (row_place == col_place).astype(jnp.float32) - 0.5 * (interior & (col_place == row_place - stride)).astype(jnp.float32) - 0.5 * (interior & (col_place == row_place + stride) & (row_place + stride < lengths[dimension])).astype(jnp.float32)
        matrix = matrix * factor
    return matrix


def inject_matrix(level_row, point_count, full_len):
    coords, lengths = mid_coords(level_row, point_count)
    target = jnp.zeros((point_count,), jnp.int32)
    for dimension in range(3):
        target = target + coords[dimension] * (full_len // lengths[dimension]) * (full_len ** (2 - dimension))
    return (jnp.arange(full_len ** 3, dtype=jnp.int32)[:, None] == target[None, :]).astype(jnp.float32)


def advance(values_now, spread_rate, drift_rate, operator):
    centre = values_now[1:-1]
    upper_side = values_now[2:]
    lower_side = values_now[:-2]
    updated = centre + spread_rate[0] * (upper_side + lower_side - 2.0 * centre) + 0.5 * drift_rate[0] * (upper_side - lower_side)
    updated = updated + jnp.einsum("pq,rql->rpl", operator, centre, precision=lax.Precision.HIGHEST)
    padded = jnp.pad(centre, ((0, 0), (0, 0), (1, 1)))
    last_len = centre.shape[2]
    upper_side = padded[:, :, 2:]
    lower_side = padded[:, :, :last_len]
    updated = updated + spread_rate[4] * (upper_side + lower_side - 2.0 * centre) + 0.5 * drift_rate[4] * (upper_side - lower_side)
    return updated


def reference(initial, diffusion, drift, levels, weights):
    grid_count = initial.shape[0]
    row_total = initial.shape[1]
    point_count = initial.shape[2]
    last_len = initial.shape[3]
    stepped_all = []
    total = jnp.zeros((row_total, MLEN ** 3, last_len), jnp.float32)
    for member in range(grid_count):
        level_row = levels[member]
        operator = mid_operator(level_row, diffusion[member], drift[member], point_count)
        values_now = initial[member]
        for step_number in range(STEPS):
            values_now = advance(jnp.pad(values_now, ((1, 1), (0, 0), (0, 0))), diffusion[member], drift[member], operator)
        stepped_all.append(values_now)
        surplus = jnp.einsum("pq,rql->rpl", mid_surplus(level_row, point_count), values_now, precision=lax.Precision.HIGHEST)
        grid_scale = weights[member].astype(jnp.float32) / grid_count
        placed = jnp.einsum("fp,rpl->rfl", inject_matrix(level_row, point_count, MLEN), surplus, precision=lax.Precision.HIGHEST)
        total = total + placed * grid_scale
    combined = total.reshape(row_total, MLEN, MLEN, MLEN, last_len)
    for dimension in range(1, 4):
        combined = along_dim(combined, nodal_matrix(MLEN), dimension)
    return jnp.stack(stepped_all), combined
```

```python
import itertools

import jax
import jax.numpy as jnp
import numpy as np
from jax import lax
from jax.experimental import pallas as pl
from jax.experimental.pallas import tpu as pltpu
from jax.sharding import PartitionSpec as P

STEPS = 4
MLEN = 8
FINEST = 3
LEVEL_SUM = 6
ZLEN = 8


def rank_of(coordinate):
    if coordinate % 4 == 0:
        return 1
    return 2 if coordinate % 2 == 0 else 3


def union_points():
    points = []
    for first in (0, 4, 2, 6, 1, 3, 5, 7):
        for second, third in itertools.product(range(MLEN), repeat=2):
            if rank_of(first) + rank_of(second) + rank_of(third) <= LEVEL_SUM:
                points.append((first, second, third))
    return np.array(points, np.int32)


POINTS = union_points()
COUNT = len(POINTS)


def nodal_matrix(length_dim):
    matrix = np.eye(length_dim)
    stride = length_dim // 2
    while stride >= 1:
        for position in range(stride, length_dim, 2 * stride):
            matrix[position] = matrix[position] + 0.5 * matrix[position - stride]
            if position + stride < length_dim:
                matrix[position] = matrix[position] + 0.5 * matrix[position + stride]
        stride = stride // 2
    return matrix


def fill_matrix():
    nodal = nodal_matrix(MLEN)
    matrix = np.zeros((MLEN, MLEN, MLEN, COUNT))
    for column, (first, second, third) in enumerate(POINTS):
        matrix[first, :, :, column] = np.outer(nodal[:, second], nodal[:, third])
    return matrix.reshape(MLEN**3, COUNT)


def split_three(values):
    high = values.astype(jnp.bfloat16)
    rest = values - high.astype(jnp.float32)
    middle = rest.astype(jnp.bfloat16)
    low = (rest - middle.astype(jnp.float32)).astype(jnp.bfloat16)
    return high, middle, low


def exact_dot(matrix, values):
    total = None
    for part in split_three(values):
        term = jnp.dot(matrix, part, preferred_element_type=jnp.float32)
        total = term if total is None else total + term
    return total


def step_kernel(
    rows, points, place_ref, level_ref, spread_ref, drift_ref, start_ref, before_ref, after_ref,
    stepped_ref, *rest
):
    parts = rest[:ZLEN]
    first, second, final, coef_ref, load_sem, store_sem = rest[ZLEN:]
    halo = STEPS
    share = rows // ZLEN
    loads = [
        pltpu.make_async_copy(before_ref, first.at[pl.ds(0, halo * points)], load_sem.at[0]),
        pltpu.make_async_copy(start_ref, first.at[pl.ds(halo * points, rows * points)], load_sem.at[1]),
        pltpu.make_async_copy(
            after_ref, first.at[pl.ds((halo + rows) * points, halo * points)], load_sem.at[2]
        ),
    ]
    for load in loads:
        load.start()

    place = lax.broadcasted_iota(jnp.int32, (points, 128), 0)
    lane = lax.broadcasted_iota(jnp.int32, (8, 128), 1)
    offsets = [level_ref[0, 1] + level_ref[0, 2], level_ref[0, 2], jnp.int32(0)]
    strides = []
    centre_rate = 1.0 - 2.0 * spread_ref[0, 0] - 2.0 * spread_ref[0, 4]
    for dim in range(3):
        length = jnp.left_shift(jnp.int32(1), level_ref[0, dim])
        coord = jnp.bitwise_and(jnp.right_shift(place, offsets[dim]), length - 1)
        spread, drift = spread_ref[0, dim + 1], 0.5 * drift_ref[0, dim + 1]
        coef_ref[2 * dim] = jnp.where(coord < length - 1, spread + drift, 0.0)
        coef_ref[2 * dim + 1] = jnp.where(coord > 0, spread - drift, 0.0)
        strides.append(jnp.left_shift(jnp.int32(1), offsets[dim]))
        centre_rate = centre_rate - 2.0 * spread
    row_up = spread_ref[0, 0] + 0.5 * drift_ref[0, 0]
    row_down = spread_ref[0, 0] - 0.5 * drift_ref[0, 0]
    lane_up = jnp.where(lane < 127, spread_ref[0, 4] + 0.5 * drift_ref[0, 4], 0.0)
    lane_down = jnp.where(lane > 0, spread_ref[0, 4] - 0.5 * drift_ref[0, 4], 0.0)
    keep_low = place_ref[1].astype(jnp.float32)
    keep_high = place_ref[2].astype(jnp.float32)

    for load in loads:
        load.wait()

    def advance(source, target, step, target_base):
        low, high = step, 2 * halo + rows - step

        def tile(tile_index, carry):
            base = pl.multiple_of(tile_index * 8, 8)
            coefs = [coef_ref[i, pl.ds(base, 8), :] for i in range(6)]

            def update(row, below, centre, above):
                offset = row * points + base
                total = centre * centre_rate + above * row_up + below * row_down
                total = total + pltpu.roll(centre, 127, 1) * lane_up
                total = total + pltpu.roll(centre, 1, 1) * lane_down
                for dim in range(3):
                    total = total + source[pl.ds(offset + strides[dim], 8), :] * coefs[2 * dim]
                    total = total + source[pl.ds(offset - strides[dim], 8), :] * coefs[2 * dim + 1]
                return total

            def store(row, value):
                offset = pl.multiple_of((row - target_base) * points + base, 8)
                target[pl.ds(offset, 8), :] = value

            def at(row):
                return source[pl.ds(pl.multiple_of(row * points + base, 8), 8), :]

            below, centre = at(low - 1), at(low)
            for row in range(low, halo):
                above = at(row + 1)
                store(row, update(row, below, centre, above) * keep_low)
                below, centre = centre, above

            def group(index, pair):
                below, centre = pair
                for k in range(8):
                    row = halo + index * 8 + k
                    above = at(row + 1)
                    store(row, update(row, below, centre, above))
                    below, centre = centre, above
                return below, centre

            below, centre = lax.fori_loop(0, rows // 8, group, (below, centre))
            for row in range(halo + rows, high):
                above = at(row + 1)
                store(row, update(row, below, centre, above) * keep_high)
                below, centre = centre, above
            return carry

        lax.fori_loop(0, points // 8, tile, 0)

    advance(first, second, 1, 0)
    advance(second, first, 2, 0)
    advance(first, second, 3, 0)
    advance(second, final, 4, halo)

    stores = [pltpu.make_async_copy(final, stepped_ref, store_sem.at[ZLEN])]
    for index, part in enumerate(parts):
        begin = pl.multiple_of(jnp.bitwise_xor(place_ref[0], index) * (share * points), 8)
        stores.append(
            pltpu.make_async_copy(final.at[pl.ds(begin, share * points)], part, store_sem.at[index])
        )
    for copy in stores:
        copy.start()
    for copy in stores:
        copy.wait()


def step_rows(place, levels, spread, drift, start, before, after):
    rows, points, lanes = start.shape
    share = rows // ZLEN * points
    flat = lambda v: v.reshape(-1, lanes)
    anywhere = pl.BlockSpec(memory_space=pl.ANY)
    scalars = pl.BlockSpec(memory_space=pltpu.SMEM)
    total = rows + 2 * STEPS
    outs = pl.pallas_call(
        lambda *refs: step_kernel(rows, points, *refs),
        out_shape=[jax.ShapeDtypeStruct((rows * points, lanes), jnp.float32)]
        + [jax.ShapeDtypeStruct((share, lanes), jnp.float32)] * ZLEN,
        in_specs=[scalars] * 4 + [anywhere] * 3,
        out_specs=[anywhere] * (1 + ZLEN),
        scratch_shapes=[
            pltpu.VMEM((total * points, lanes), jnp.float32),
            pltpu.VMEM((total * points, lanes), jnp.float32),
            pltpu.VMEM((rows * points, lanes), jnp.float32),
            pltpu.VMEM((6, points, lanes), jnp.float32),
            pltpu.SemaphoreType.DMA((3,)),
            pltpu.SemaphoreType.DMA((ZLEN + 1,)),
        ],
        compiler_params=pltpu.CompilerParams(vmem_limit_bytes=24 * 2**20),
        cost_estimate=pl.CostEstimate(
            flops=25 * STEPS * total * points * lanes, bytes_accessed=16 * rows * points * lanes,
            transcendentals=0,
        ),
        name="step_rows",
    )(place, levels, spread, drift, flat(start), flat(before), flat(after))
    return outs[0].reshape(rows, points, lanes), outs[1:]


def combine_kernel(share, points, matrix_ref, *refs):
    out_ref = refs[-1]
    matrix = matrix_ref[...]
    for row in range(share):
        stack = [ref[row * points : (row + 1) * points, :] for ref in refs[:-1]]
        out_ref[row] = exact_dot(matrix, jnp.concatenate(stack, axis=0))


def combine(matrix, pieces, share):
    lanes = pieces[0].shape[1]
    points = pieces[0].shape[0] // share
    return pl.pallas_call(
        lambda *refs: combine_kernel(share, points, *refs),
        out_shape=jax.ShapeDtypeStruct((share, COUNT, lanes), jnp.float32),
        compiler_params=pltpu.CompilerParams(vmem_limit_bytes=24 * 2**20),
        cost_estimate=pl.CostEstimate(
            flops=6 * share * matrix.size * lanes, bytes_accessed=4 * 2**20, transcendentals=0
        ),
        name="combine",
    )(matrix, *pieces)


def fill_kernel(chunks, width, with_base, where_ref, matrix_ref, *refs):
    sources = refs[:chunks]
    out_ref, scratch, sems = refs[chunks + with_base :]
    matrix = matrix_ref[...]
    copies = []
    points = MLEN**2
    for index, source in enumerate(sources):
        for row in range(width):
            flat = exact_dot(matrix, source[row])
            at = lambda c: flat[c * points : (c + 1) * points]
            nodal = [None] * MLEN
            nodal[0] = at(0)
            nodal[4] = at(4) + 0.5 * nodal[0]
            nodal[2] = at(2) + 0.5 * (nodal[0] + nodal[4])
            nodal[6] = at(6) + 0.5 * nodal[4]
            nodal[1] = at(1) + 0.5 * (nodal[0] + nodal[2])
            nodal[3] = at(3) + 0.5 * (nodal[2] + nodal[4])
            nodal[5] = at(5) + 0.5 * (nodal[4] + nodal[6])
            nodal[7] = at(7) + 0.5 * nodal[6]
            for c in range(MLEN):
                scratch[index * width + row, c * points : (c + 1) * points, :] = nodal[c]
        copy = pltpu.make_async_copy(
            scratch.at[pl.ds(index * width, width)],
            out_ref.at[pl.ds(where_ref[index], width)],
            sems.at[index],
        )
        copy.start()
        copies.append(copy)
    for copy in copies:
        copy.wait()


def fill(where, matrix, sources, rows, base):
    width, _, lanes = sources[0].shape
    chunks = len(sources)
    with_base = 0 if base is None else 1
    args = [where, matrix, *sources] + ([base] if with_base else [])
    anywhere = pl.BlockSpec(memory_space=pl.ANY)
    vector = pl.BlockSpec(memory_space=pltpu.VMEM)
    return pl.pallas_call(
        lambda *refs: fill_kernel(chunks, width, with_base, *refs),
        out_shape=jax.ShapeDtypeStruct((rows, MLEN**3, lanes), jnp.float32),
        in_specs=[pl.BlockSpec(memory_space=pltpu.SMEM)] + [vector] * (1 + chunks) + [anywhere] * with_base,
        out_specs=anywhere,
        input_output_aliases={2 + chunks: 0} if with_base else {},
        scratch_shapes=[
            pltpu.VMEM((chunks * width, MLEN**3, lanes), jnp.float32),
            pltpu.SemaphoreType.DMA((chunks,)),
        ],
        compiler_params=pltpu.CompilerParams(vmem_limit_bytes=24 * 2**20),
        cost_estimate=pl.CostEstimate(
            flops=6 * chunks * width * matrix.size * lanes,
            bytes_accessed=4 * chunks * width * (MLEN**3 + COUNT) * lanes,
            transcendentals=0,
        ),
        name="fill",
    )(*args)


def placing_matrix(levels, scale, point_count):
    grids = levels.shape[0]
    shape = (COUNT, grids * point_count)
    column = lax.broadcasted_iota(jnp.int32, shape, 1) % point_count
    spread = lambda v: jnp.repeat(v, point_count)[None, :]
    level = [spread(levels[:, dim]) for dim in range(3)]
    offsets = [level[1] + level[2], level[2], jnp.zeros_like(level[0])]
    matrix = jnp.broadcast_to(spread(scale), shape)
    for dim in range(3):
        length = jnp.left_shift(jnp.ones_like(level[dim]), level[dim])
        coord = jnp.bitwise_and(jnp.right_shift(column, offsets[dim]), length - 1)
        shift = FINEST - level[dim]
        target = jnp.asarray(POINTS[:, dim])[:, None]
        row = jnp.right_shift(target, shift)
        present = jnp.left_shift(row, shift) == target
        stride = jnp.bitwise_and(row, -row)
        near = (row > 0) & ((coord == row - stride) | (coord == row + stride))
        factor = (coord == row).astype(jnp.float32) - 0.5 * near.astype(jnp.float32)
        matrix = matrix * jnp.where(present, factor, 0.0)
    return matrix.astype(jnp.bfloat16)


def per_device(initial, diffusion, drift, levels, weights):
    values = initial[0]
    rows, points, _ = values.shape
    share = rows // ZLEN
    dom_size = lax.axis_size("dom")
    grid_size = lax.axis_size("grid")
    columns = grid_size // ZLEN
    dom = lax.axis_index("dom")
    grid = lax.axis_index("grid")
    z, y = grid // columns, grid % columns

    facts = lax.all_gather(jnp.concatenate([levels[0], weights]), "grid")

    up = [(i, i + 1) for i in range(dom_size - 1)]
    down = [(j, i) for i, j in up]
    before = lax.ppermute(values[rows - STEPS :], "dom", up)
    after = lax.ppermute(values[:STEPS], "dom", down)
    place = jnp.stack([z, (dom > 0).astype(jnp.int32), (dom < dom_size - 1).astype(jnp.int32)])
    stepped, parts = step_rows(place, levels, diffusion, drift, values, before, after)

    pieces = [parts[0]] + [
        lax.ppermute(parts[k], "grid", [(i, i ^ (k * columns)) for i in range(grid_size)])
        for k in range(1, ZLEN)
    ]
    members = jnp.bitwise_xor(z, jnp.arange(ZLEN, dtype=jnp.int32)) * columns + y
    chosen = facts[members]
    matrix = placing_matrix(chosen[:, :3], chosen[:, 3].astype(jnp.float32) / grid_size, points)
    partial = combine(matrix, pieces, share)
    other = lax.ppermute(partial, "grid", [(i, i ^ 1) for i in range(grid_size)])
    half = share // 2
    ups = [partial[:half] + other[:half], partial[half:] + other[half:]]
    downs = list(ups)

    plus = [(i, (i + columns) % grid_size) for i in range(grid_size)]
    minus = [(j, i) for i, j in plus]
    matrix = jnp.asarray(fill_matrix(), jnp.bfloat16)
    begin = lambda source, part: source % ZLEN * share + part * half
    combined = fill(jnp.stack([begin(z, 0), begin(z, 1)]), matrix, ups, rows, None)
    for hop in range(1, ZLEN // 2):
        ups = [lax.ppermute(v, "grid", plus) for v in ups]
        downs = [lax.ppermute(v, "grid", minus) for v in downs]
        where = jnp.stack(
            [begin(z - hop + ZLEN, s) for s in range(2)] + [begin(z + hop, s) for s in range(2)]
        )
        combined = fill(where, matrix, ups + downs, rows, combined)
    last = [lax.ppermute(ups[0], "grid", plus), lax.ppermute(downs[1], "grid", minus)]
    where = jnp.stack([begin(z + ZLEN // 2, s) for s in range(2)])
    combined = fill(where, matrix, last, rows, combined)
    return stepped[None], combined.reshape(rows, MLEN, MLEN, MLEN, -1)


def solution(mesh):
    in_specs = (
        P("grid", "dom", None, None),
        P("grid", None),
        P("grid", None),
        P("grid", None),
        P("grid"),
    )
    out_specs = (P("grid", "dom", None, None), P("dom", None, None, None, None))
    return jax.shard_map(
        per_device, mesh=mesh, in_specs=in_specs, out_specs=out_specs, check_vma=False
    )
```

```python
import itertools

import jax
import jax.numpy as jnp
import numpy as np
from jax import lax
from jax.experimental import pallas as pl
from jax.experimental.pallas import tpu as pltpu
from jax.sharding import PartitionSpec as P

STEPS = 4
MLEN = 8
FINEST = 3
LEVEL_SUM = 6
ZLEN = 8


def rank_of(coordinate):
    if coordinate % 4 == 0:
        return 1
    return 2 if coordinate % 2 == 0 else 3


def union_points():
    points = []
    for first in (0, 4, 2, 6, 1, 3, 5, 7):
        for second, third in itertools.product(range(MLEN), repeat=2):
            if rank_of(first) + rank_of(second) + rank_of(third) <= LEVEL_SUM:
                points.append((first, second, third))
    return np.array(points, np.int32)


POINTS = union_points()
COUNT = len(POINTS)
SUB = 64
META = 8
TRIPLES = ((1, 2), (1, 3), (2, 1), (2, 2), (2, 3), (3, 1), (3, 2))
GROUPS = (((0, 48), (0,)), ((48, 96), (4,)), ((96, 160), (2, 6)), ((160, 208), (1, 3, 5, 7)))


def nodal_matrix(length_dim):
    matrix = np.eye(length_dim)
    stride = length_dim // 2
    while stride >= 1:
        for position in range(stride, length_dim, 2 * stride):
            matrix[position] = matrix[position] + 0.5 * matrix[position - stride]
            if position + stride < length_dim:
                matrix[position] = matrix[position] + 0.5 * matrix[position + stride]
        stride = stride // 2
    return matrix


def fill_matrix():
    nodal = nodal_matrix(MLEN)
    square = MLEN**2
    matrix = np.zeros((MLEN, MLEN, MLEN, COUNT))
    for column, (first, second, third) in enumerate(POINTS):
        matrix[first, :, :, column] = np.outer(nodal[:, second], nodal[:, third])
    matrix = matrix.reshape(MLEN, square, COUNT)
    packed = np.zeros((MLEN * square, 256))
    begin = 0
    for (low, high), members in GROUPS:
        block = matrix[list(members), :, low:high].reshape(-1, high - low)
        packed[begin : begin + len(block), : 3 * (high - low)] = np.tile(block, (1, 3))
        begin += len(block)
    return packed

def placing_table():
    tables = []
    for first, second in TRIPLES:
        level = (first, second, LEVEL_SUM - first - second)
        length = [2**v for v in level]
        surplus = np.ones((1, 1))
        for n in length:
            surplus = np.kron(surplus, np.round(2.0 * np.linalg.inv(nodal_matrix(n))) / 2.0)
        target = np.zeros((COUNT, SUB))
        for column, coords in enumerate(itertools.product(*[range(n) for n in length])):
            point = [c * (MLEN // n) for c, n in zip(coords, length)]
            target[np.all(POINTS == point, axis=1), column] = 1.0
        tables.append(np.tile(target @ surplus, (1, 3)))
    return np.stack(tables)


def split_three(values):
    high = values.astype(jnp.bfloat16)
    rest = values - high.astype(jnp.float32)
    middle = rest.astype(jnp.bfloat16)
    low = (rest - middle.astype(jnp.float32)).astype(jnp.bfloat16)
    return high, middle, low


def step_kernel(rows, points, facts_ref, start_ref, before_ref, after_ref, stepped_ref, *rest):
    parts = rest[: 2 * ZLEN]
    first, second, final, coef_ref, load_sem, store_sem = rest[2 * ZLEN :]
    halo = STEPS
    share = rows // ZLEN
    half = share // 2 * points
    block = 2 * half + META
    loads = [
        pltpu.make_async_copy(before_ref, first.at[pl.ds(0, halo * points)], load_sem.at[0]),
        pltpu.make_async_copy(start_ref, first.at[pl.ds(halo * points, rows * points)], load_sem.at[1]),
        pltpu.make_async_copy(
            after_ref, first.at[pl.ds((halo + rows) * points, halo * points)], load_sem.at[2]
        ),
    ]
    for load in loads:
        load.start()

    member = facts_ref[0].astype(jnp.int32)
    keep_low, keep_high = facts_ref[1], facts_ref[2]
    levels = [facts_ref[3 + dim].astype(jnp.int32) for dim in range(3)]
    weight = facts_ref[6]
    spread = [facts_ref[7 + dim] for dim in range(5)]
    drift = [0.5 * facts_ref[12 + dim] for dim in range(5)]

    place = lax.broadcasted_iota(jnp.int32, (points, 128), 0)
    lane = lax.broadcasted_iota(jnp.int32, (8, 128), 1)
    sublane = lax.broadcasted_iota(jnp.int32, (META, 128), 0)
    offsets = [levels[1] + levels[2], levels[2], jnp.int32(0)]
    strides = []
    centre_rate = 1.0 - 2.0 * spread[0] - 2.0 * spread[4]
    for dim in range(3):
        length = jnp.left_shift(jnp.int32(1), levels[dim])
        coord = jnp.bitwise_and(jnp.right_shift(place, offsets[dim]), length - 1)
        coef_ref[2 * dim] = jnp.where(coord < length - 1, spread[dim + 1] + drift[dim + 1], 0.0)
        coef_ref[2 * dim + 1] = jnp.where(coord > 0, spread[dim + 1] - drift[dim + 1], 0.0)
        strides.append(jnp.left_shift(jnp.int32(1), offsets[dim]))
        centre_rate = centre_rate - 2.0 * spread[dim + 1]
    row_up, row_down = spread[0] + drift[0], spread[0] - drift[0]
    lane_up = jnp.where(lane < 127, spread[4] + drift[4], 0.0)
    lane_down = jnp.where(lane > 0, spread[4] - drift[4], 0.0)
    triple = (3 * levels[0] + levels[1] - 5).astype(jnp.float32)
    for group in range(ZLEN):
        final[group * block + half : group * block + half + META, :] = jnp.where(
            sublane == 0, triple, weight
        )

    for load in loads:
        load.wait()

    def advance(source, target, step, locate):
        low, high = step, 2 * halo + rows - step

        def tile(tile_index, carry):
            base = pl.multiple_of(tile_index * 8, 8)
            coefs = [coef_ref[i, pl.ds(base, 8), :] for i in range(6)]

            def at(row):
                return source[pl.ds(pl.multiple_of(row * points + base, 8), 8), :]

            below, centre = at(low - 1), at(low)
            for row in range(low, high):
                above = at(row + 1)
                offset = row * points + base
                total = centre * centre_rate + above * row_up + below * row_down
                total = total + pltpu.roll(centre, 127, 1) * lane_up
                total = total + pltpu.roll(centre, 1, 1) * lane_down
                for dim in range(3):
                    total = total + source[pl.ds(offset + strides[dim], 8), :] * coefs[2 * dim]
                    total = total + source[pl.ds(offset - strides[dim], 8), :] * coefs[2 * dim + 1]
                if row < halo:
                    total = total * keep_low
                if row >= halo + rows:
                    total = total * keep_high
                target[pl.ds(pl.multiple_of(locate(row) + base, 8), 8), :] = total
                below, centre = centre, above
            return carry

        lax.fori_loop(0, points // 8, tile, 0, unroll=2)

    def located(row):
        group, inner = divmod(row - halo, share)
        return group * block + inner * points + (META if inner >= share // 2 else 0)

    advance(first, second, 1, lambda row: row * points)
    advance(second, first, 2, lambda row: row * points)
    advance(first, second, 3, lambda row: row * points)
    advance(second, final, 4, located)

    stores = []
    for index in range(ZLEN):
        begin = pl.multiple_of(jnp.bitwise_xor(member, index) * block, 8)
        stores.append((final.at[pl.ds(begin, half + META)], parts[index]))
    for index in range(ZLEN):
        begin = pl.multiple_of(jnp.bitwise_xor(member, index) * block + half + META, 8)
        stores.append((final.at[pl.ds(begin, half)], parts[ZLEN + index]))
    for index in range(2 * ZLEN):
        begin = index // 2 * block + index % 2 * (half + META)
        stores.append(
            (final.at[pl.ds(begin, half)], stepped_ref.at[pl.ds(index * half, half)])
        )
    copies = [
        pltpu.make_async_copy(source, target, store_sem.at[index])
        for index, (source, target) in enumerate(stores)
    ]
    for copy in copies:
        copy.start()
    for copy in copies:
        copy.wait()


def step_rows(facts, start, before, after):
    rows, points, lanes = start.shape
    half = rows // ZLEN // 2 * points
    flat = lambda v: v.reshape(-1, lanes)
    anywhere = pl.BlockSpec(memory_space=pl.ANY)
    total = rows + 2 * STEPS
    outs = pl.pallas_call(
        lambda *refs: step_kernel(rows, points, *refs),
        out_shape=[jax.ShapeDtypeStruct((rows * points, lanes), jnp.float32)]
        + [jax.ShapeDtypeStruct((half + META, lanes), jnp.float32)] * ZLEN
        + [jax.ShapeDtypeStruct((half, lanes), jnp.float32)] * ZLEN,
        in_specs=[pl.BlockSpec(memory_space=pltpu.SMEM)] + [anywhere] * 3,
        out_specs=[anywhere] * (1 + 2 * ZLEN),
        scratch_shapes=[
            pltpu.VMEM((total * points, lanes), jnp.float32),
            pltpu.VMEM((total * points, lanes), jnp.float32),
            pltpu.VMEM((ZLEN * (2 * half + META), lanes), jnp.float32),
            pltpu.VMEM((6, points, lanes), jnp.float32),
            pltpu.SemaphoreType.DMA((3,)),
            pltpu.SemaphoreType.DMA((4 * ZLEN,)),
        ],
        compiler_params=pltpu.CompilerParams(vmem_limit_bytes=24 * 2**20),
        cost_estimate=pl.CostEstimate(
            flops=25 * STEPS * total * points * lanes, bytes_accessed=16 * rows * points * lanes,
            transcendentals=0,
        ),
        name="step_rows",
    )(facts, flat(start), flat(before), flat(after))
    return outs[0].reshape(rows, points, lanes), outs[1 : 1 + ZLEN], outs[1 + ZLEN :]


def combine_kernel(grids, table_ref, *refs):
    headed, pieces, out_ref = refs[:ZLEN], refs[:-1][-ZLEN:], refs[-1]
    width, _, lanes = out_ref.shape
    half = width * SUB
    total = None
    for head, piece in zip(headed, pieces):
        triple = jnp.clip(jnp.max(head[half : half + 1, :]).astype(jnp.int32), 0, len(TRIPLES) - 1)
        scale = jnp.max(head[half + 1 : half + 2, :]) / grids
        wide = jnp.concatenate([piece[r * SUB : (r + 1) * SUB, :] for r in range(width)], axis=1)
        stack = jnp.concatenate(split_three(wide * scale), axis=0)
        term = jnp.dot(table_ref[triple], stack, preferred_element_type=jnp.float32)
        total = term if total is None else total + term
    for row in range(width):
        out_ref[row] = total[:, row * lanes : (row + 1) * lanes]


def combine(table, headed, pieces, width, grids):
    lanes = headed[0].shape[1]
    arrays = list(headed) + ([] if pieces is None else list(pieces))
    return pl.pallas_call(
        lambda *refs: combine_kernel(grids, *refs),
        out_shape=jax.ShapeDtypeStruct((width, COUNT, lanes), jnp.float32),
        compiler_params=pltpu.CompilerParams(vmem_limit_bytes=24 * 2**20),
        cost_estimate=pl.CostEstimate(
            flops=2 * ZLEN * 3 * SUB * COUNT * width * lanes, bytes_accessed=2**20, transcendentals=0
        ),
        name="combine",
    )(table, *arrays)


def fill_kernel(chunks, width, with_base, where_ref, matrix_ref, *refs):
    sources = refs[:chunks]
    out_ref, scratch, sems = refs[chunks + with_base :]
    square = MLEN**2
    copies = []
    for index, source in enumerate(sources):
        lanes = source.shape[2]
        parts = split_three(jnp.concatenate([source[row] for row in range(width)], axis=1))
        level = {}
        begin = 0
        for (low, high), members in GROUPS:
            block = matrix_ref[begin : begin + square * len(members), : 3 * (high - low)]
            stack = jnp.concatenate([part[low:high] for part in parts], axis=0)
            result = jnp.dot(block, stack, preferred_element_type=jnp.float32)
            for k, member in enumerate(members):
                level[member] = result[k * square : (k + 1) * square]
            begin += square * len(members)
        nodal = dict(level)
        nodal[4] = level[4] + 0.5 * nodal[0]
        nodal[2] = level[2] + 0.5 * (nodal[0] + nodal[4])
        nodal[6] = level[6] + 0.5 * nodal[4]
        for odd in (1, 3, 5):
            nodal[odd] = level[odd] + 0.5 * (nodal[odd - 1] + nodal[odd + 1])
        nodal[7] = level[7] + 0.5 * nodal[6]
        for row in range(width):
            for c in range(MLEN):
                scratch[index * width + row, c * square : (c + 1) * square, :] = nodal[c][
                    :, row * lanes : (row + 1) * lanes
                ]
        copy = pltpu.make_async_copy(
            scratch.at[pl.ds(index * width, width)],
            out_ref.at[pl.ds(where_ref[index], width)],
            sems.at[index],
        )
        copy.start()
        copies.append(copy)
    for copy in copies:
        copy.wait()


def fill(where, matrix, sources, rows, base):
    width, _, lanes = sources[0].shape
    chunks = len(sources)
    with_base = 0 if base is None else 1
    args = [where, matrix, *sources] + ([base] if with_base else [])
    anywhere = pl.BlockSpec(memory_space=pl.ANY)
    vector = pl.BlockSpec(memory_space=pltpu.VMEM)
    return pl.pallas_call(
        lambda *refs: fill_kernel(chunks, width, with_base, *refs),
        out_shape=jax.ShapeDtypeStruct((rows, MLEN**3, lanes), jnp.float32),
        in_specs=[pl.BlockSpec(memory_space=pltpu.SMEM)] + [vector] * (1 + chunks) + [anywhere] * with_base,
        out_specs=anywhere,
        input_output_aliases={2 + chunks: 0} if with_base else {},
        scratch_shapes=[
            pltpu.VMEM((chunks * width, MLEN**3, lanes), jnp.float32),
            pltpu.SemaphoreType.DMA((chunks,)),
        ],
        compiler_params=pltpu.CompilerParams(vmem_limit_bytes=24 * 2**20),
        cost_estimate=pl.CostEstimate(
            flops=6 * chunks * width * matrix.size * lanes,
            bytes_accessed=4 * chunks * width * (MLEN**3 + COUNT) * lanes,
            transcendentals=0,
        ),
        name="fill",
    )(*args)


def per_device(initial, diffusion, drift, levels, weights):
    values = initial[0]
    rows, points, _ = values.shape
    share = rows // ZLEN
    half = share // 2
    dom_size = lax.axis_size("dom")
    grid_size = lax.axis_size("grid")
    columns = grid_size // ZLEN
    dom = lax.axis_index("dom")
    z = lax.axis_index("grid") // columns
    swap = lambda v, bits: lax.ppermute(v, "grid", [(i, i ^ bits) for i in range(grid_size)])

    up = [(i, i + 1) for i in range(dom_size - 1)]
    down = [(j, i) for i, j in up]
    before = lax.ppermute(values[rows - STEPS :], "dom", up)
    after = lax.ppermute(values[:STEPS], "dom", down)
    place = jnp.stack([z, (dom > 0).astype(jnp.int32), (dom < dom_size - 1).astype(jnp.int32)])
    facts = jnp.concatenate([place, levels[0], weights]).astype(jnp.float32)
    facts = jnp.concatenate([facts, diffusion[0], drift[0]])
    stepped, headed, others = step_rows(facts, values, before, after)

    headed = [headed[0]] + [swap(headed[k], k * columns) for k in range(1, ZLEN)]
    others = [others[0]] + [swap(others[k], k * columns) for k in range(1, ZLEN)]
    table = jnp.asarray(placing_table(), jnp.bfloat16)
    sums = []
    for pieces in (None, others):
        partial = combine(table, headed, pieces, half, grid_size)
        sums.append(partial + swap(partial, 1))

    plus = [(i, (i + columns) % grid_size) for i in range(grid_size)]
    minus = [(j, i) for i, j in plus]
    matrix = jnp.asarray(fill_matrix(), jnp.bfloat16)
    begin = lambda source, part: source % ZLEN * share + part * half
    ups, downs = sums, sums
    chunks, where = list(sums), [begin(z, 0), begin(z, 1)]
    combined = None
    for hop in range(1, ZLEN // 2):
        next_ups = [lax.ppermute(v, "grid", plus) for v in ups]
        next_downs = [lax.ppermute(v, "grid", minus) for v in downs]
        if hop > 1:
            combined = fill(jnp.stack(where), matrix, chunks, rows, combined)
            chunks, where = [], []
            next_ups, next_downs, combined = lax.optimization_barrier(
                (next_ups, next_downs, combined)
            )
        ups, downs = next_ups, next_downs
        chunks = chunks + ups + downs
        where = where + [begin(z - hop + ZLEN, s) for s in range(2)]
        where = where + [begin(z + hop, s) for s in range(2)]
    last = [lax.ppermute(ups[0], "grid", plus), lax.ppermute(downs[1], "grid", minus)]
    combined = fill(jnp.stack(where), matrix, chunks, rows, combined)
    last, combined = lax.optimization_barrier((last, combined))
    where = [begin(z + ZLEN // 2, s) for s in range(2)]
    combined = fill(jnp.stack(where), matrix, last, rows, combined)
    return stepped[None], combined.reshape(rows, MLEN, MLEN, MLEN, -1)


def solution(mesh):
    in_specs = (
        P("grid", "dom", None, None),
        P("grid", None),
        P("grid", None),
        P("grid", None),
        P("grid"),
    )
    out_specs = (P("grid", "dom", None, None), P("dom", None, None, None, None))
    return jax.shard_map(
        per_device, mesh=mesh, in_specs=in_specs, out_specs=out_specs, check_vma=False
    )
```

```python
import itertools

import jax
import jax.numpy as jnp
import numpy as np
from jax import lax
from jax.experimental import pallas as pl
from jax.experimental.pallas import tpu as pltpu
from jax.sharding import PartitionSpec as P

STEPS = 4
MLEN = 8
FINEST = 3
LEVEL_SUM = 6
ZLEN = 8
QUARTERS = 4
ORDER = (2, 1, 3)
INNER_LIMIT = 24 * 2**20
OUTER_LIMIT = 24 * 2**20


def rank_of(coordinate):
    if coordinate % 4 == 0:
        return 1
    return 2 if coordinate % 2 == 0 else 3


def union_points():
    points = []
    for first in (0, 4, 2, 6, 1, 3, 5, 7):
        for second, third in itertools.product(range(MLEN), repeat=2):
            if rank_of(first) + rank_of(second) + rank_of(third) <= LEVEL_SUM:
                points.append((first, second, third))
    return np.array(points, np.int32)


POINTS = union_points()
COUNT = len(POINTS)
SUB = 64
META = 8
TRIPLES = ((1, 2), (1, 3), (2, 1), (2, 2), (2, 3), (3, 1), (3, 2))
GROUPS = (((0, 48), (0,)), ((48, 96), (4,)), ((96, 160), (2, 6)), ((160, 208), (1, 3, 5, 7)))


def nodal_matrix(length_dim):
    matrix = np.eye(length_dim)
    stride = length_dim // 2
    while stride >= 1:
        for position in range(stride, length_dim, 2 * stride):
            matrix[position] = matrix[position] + 0.5 * matrix[position - stride]
            if position + stride < length_dim:
                matrix[position] = matrix[position] + 0.5 * matrix[position + stride]
        stride = stride // 2
    return matrix


def fill_matrix():
    nodal = nodal_matrix(MLEN)
    square = MLEN**2
    matrix = np.zeros((MLEN, MLEN, MLEN, COUNT))
    for column, (first, second, third) in enumerate(POINTS):
        matrix[first, :, :, column] = np.outer(nodal[:, second], nodal[:, third])
    matrix = matrix.reshape(MLEN, square, COUNT)
    packed = np.zeros((MLEN * square, 256))
    begin = 0
    for (low, high), members in GROUPS:
        block = matrix[list(members), :, low:high].reshape(-1, high - low)
        packed[begin : begin + len(block), : 3 * (high - low)] = np.tile(block, (1, 3))
        begin += len(block)
    return packed

def placing_table():
    tables = []
    for first, second in TRIPLES:
        level = (first, second, LEVEL_SUM - first - second)
        length = [2**v for v in level]
        surplus = np.ones((1, 1))
        for n in length:
            surplus = np.kron(surplus, np.round(2.0 * np.linalg.inv(nodal_matrix(n))) / 2.0)
        target = np.zeros((COUNT, SUB))
        for column, coords in enumerate(itertools.product(*[range(n) for n in length])):
            point = [c * (MLEN // n) for c, n in zip(coords, length)]
            target[np.all(POINTS == point, axis=1), column] = 1.0
        tables.append(np.tile(target @ surplus, (1, 3)))
    return np.stack(tables)


def split_three(values):
    high = values.astype(jnp.bfloat16)
    rest = values - high.astype(jnp.float32)
    middle = rest.astype(jnp.bfloat16)
    low = (rest - middle.astype(jnp.float32)).astype(jnp.bfloat16)
    return high, middle, low


class Stencil:
    def __init__(self, points, facts_ref, coef_ref):
        self.points, self.coef_ref = points, coef_ref
        levels = [facts_ref[dim].astype(jnp.int32) for dim in range(3)]
        spread = [facts_ref[4 + dim] for dim in range(5)]
        drift = [0.5 * facts_ref[9 + dim] for dim in range(5)]
        place = lax.broadcasted_iota(jnp.int32, (points, 128), 0)
        lane = lax.broadcasted_iota(jnp.int32, (8, 128), 1)
        sublane = lax.broadcasted_iota(jnp.int32, (META, 128), 0)
        offsets = [levels[1] + levels[2], levels[2], jnp.int32(0)]
        self.strides = []
        self.centre_rate = 1.0 - 2.0 * spread[0] - 2.0 * spread[4]
        for dim in range(3):
            length = jnp.left_shift(jnp.int32(1), levels[dim])
            coord = jnp.bitwise_and(jnp.right_shift(place, offsets[dim]), length - 1)
            rise, fall = spread[dim + 1] + drift[dim + 1], spread[dim + 1] - drift[dim + 1]
            coef_ref[2 * dim] = jnp.where(coord < length - 1, rise, 0.0)
            coef_ref[2 * dim + 1] = jnp.where(coord > 0, fall, 0.0)
            self.strides.append(jnp.left_shift(jnp.int32(1), offsets[dim]))
            self.centre_rate = self.centre_rate - 2.0 * spread[dim + 1]
        self.row_up, self.row_down = spread[0] + drift[0], spread[0] - drift[0]
        self.lane_up = jnp.where(lane < 127, spread[4] + drift[4], 0.0)
        self.lane_down = jnp.where(lane > 0, spread[4] - drift[4], 0.0)
        triple = (3 * levels[0] + levels[1] - 5).astype(jnp.float32)
        self.head = jnp.where(sublane == 0, triple, facts_ref[3])

    def advance(self, source, target, spans, locate, mask):
        points = self.points

        def tile(tile_index, carry):
            base = pl.multiple_of(tile_index * 8, 8)
            coefs = [self.coef_ref[i, pl.ds(base, 8), :] for i in range(6)]

            def at(row):
                return source[pl.ds(pl.multiple_of(row * points + base, 8), 8), :]

            for low, high in spans:
                below, centre = at(low - 1), at(low)
                for row in range(low, high):
                    above = at(row + 1)
                    offset = row * points + base
                    total = centre * self.centre_rate + above * self.row_up + below * self.row_down
                    total = total + pltpu.roll(centre, 127, 1) * self.lane_up
                    total = total + pltpu.roll(centre, 1, 1) * self.lane_down
                    for dim in range(3):
                        stride = self.strides[dim]
                        total = total + source[pl.ds(offset + stride, 8), :] * coefs[2 * dim]
                        total = total + source[pl.ds(offset - stride, 8), :] * coefs[2 * dim + 1]
                    total = mask(row, total)
                    target[pl.ds(pl.multiple_of(locate(row) + base, 8), 8), :] = total
                    below, centre = centre, above
            return carry

        lax.fori_loop(0, points // 8, tile, 0, unroll=4)


def shifted_place():
    columns = lax.axis_size("grid") // ZLEN
    core = jnp.bitwise_and(lax.axis_index("dom"), 1)
    return jnp.bitwise_and(lax.axis_index("grid") // columns - core + ZLEN, ZLEN - 1)


def inner_kernel(rows, points, facts_ref, start_ref, stepped_ref, *rest):
    parts = rest[:QUARTERS]
    first, second, final, coef_ref, load_sem, part_sem, store_sem = rest[QUARTERS:]
    share = (rows - 2 * STEPS) // QUARTERS
    size = share * points
    block = size + META
    load = pltpu.make_async_copy(start_ref, first, load_sem)
    load.start()
    quarter = jnp.right_shift(shifted_place(), 1)
    stencil = Stencil(points, facts_ref, coef_ref)
    for index in range(QUARTERS):
        final[index * block + size : (index + 1) * block, :] = stencil.head
    load.wait()

    def located(row):
        group, inner = divmod(row - STEPS, share)
        return group * block + inner * points

    same = lambda row: row * points
    keep = lambda row, value: value
    buffers = [first, second, first, second, final]
    for step in range(1, STEPS + 1):
        place = located if step == STEPS else same
        stencil.advance(buffers[step - 1], buffers[step], [(step, rows - step)], place, keep)

    copies = []
    for index, part in enumerate(parts):
        begin = pl.multiple_of(jnp.bitwise_xor(quarter, index) * block, 8)
        copies.append(
            pltpu.make_async_copy(final.at[pl.ds(begin, block)], part, part_sem.at[index])
        )
    for index in range(QUARTERS):
        copies.append(
            pltpu.make_async_copy(
                final.at[pl.ds(index * block, size)],
                stepped_ref.at[pl.ds(STEPS * points + index * size, size)],
                store_sem.at[index],
            )
        )
    for copy in copies:
        copy.start()
    for copy in copies:
        copy.wait()


def outer_kernel(rows, points, facts_ref, start_ref, before_ref, after_ref, _, stepped_ref, *rest):
    parts = rest[:QUARTERS]
    first, second, final, coef_ref, load_sem, part_sem, store_sem = rest[QUARTERS:]
    halo, near = STEPS * points, 2 * STEPS * points
    sides = [
        (before_ref, 0, halo),
        (start_ref.at[pl.ds(0, near)], halo, near),
        (start_ref.at[pl.ds(rows * points - near, near)], halo + near, near),
        (after_ref, halo + 2 * near, halo),
    ]
    loads = [
        pltpu.make_async_copy(source, first.at[pl.ds(begin, size)], load_sem.at[i])
        for i, (source, begin, size) in enumerate(sides)
    ]
    for load in loads:
        load.start()
    quarter = jnp.right_shift(shifted_place(), 1)
    dom = lax.axis_index("dom")
    keep_low = (dom > 0).astype(jnp.float32)
    keep_high = (dom < lax.axis_size("dom") - 1).astype(jnp.float32)
    stencil = Stencil(points, facts_ref, coef_ref)
    for load in loads:
        load.wait()

    strip = 3 * STEPS

    def mask(row, value):
        if row < STEPS:
            return value * keep_low
        if row >= 2 * strip - STEPS:
            return value * keep_high
        return value

    def located(row):
        side, inner = divmod(row, strip)
        return (2 * (inner - STEPS) + side) * points

    same = lambda row: row * points
    buffers = [first, second, first, second, final]
    for step in range(1, STEPS + 1):
        place = located if step == STEPS else same
        spans = [(step, strip - step), (strip + step, 2 * strip - step)]
        stencil.advance(buffers[step - 1], buffers[step], spans, place, mask)

    copies = []
    for index, part in enumerate(parts):
        begin = pl.multiple_of(jnp.bitwise_xor(quarter, index) * (2 * points), 8)
        copies.append(
            pltpu.make_async_copy(final.at[pl.ds(begin, 2 * points)], part, part_sem.at[index])
        )
    for index in range(2 * QUARTERS):
        row = index // 2 + index % 2 * (rows - STEPS)
        copies.append(
            pltpu.make_async_copy(
                final.at[pl.ds(index * points, points)],
                stepped_ref.at[pl.ds(row * points, points)],
                store_sem.at[index],
            )
        )
    for copy in copies:
        copy.start()
    for copy in copies:
        copy.wait()


def step_call(kernel, name, facts, inputs, olds, rows, points, tall, wide, part, limit):
    lanes = inputs[0].shape[-1]
    anywhere = pl.BlockSpec(memory_space=pl.ANY)
    buffer = pltpu.VMEM((tall * points, lanes), jnp.float32)
    return pl.pallas_call(
        lambda *refs: kernel(rows, points, *refs),
        out_shape=[jax.ShapeDtypeStruct((rows * points, lanes), jnp.float32)]
        + [jax.ShapeDtypeStruct((part, lanes), jnp.float32)] * QUARTERS,
        in_specs=[pl.BlockSpec(memory_space=pltpu.SMEM)] + [anywhere] * (len(inputs) + len(olds)),
        out_specs=[anywhere] * (1 + QUARTERS),
        input_output_aliases={1 + len(inputs): 0} if olds else {},
        scratch_shapes=[
            buffer,
            buffer,
            pltpu.VMEM((wide, lanes), jnp.float32),
            pltpu.VMEM((6, points, lanes), jnp.float32),
            pltpu.SemaphoreType.DMA((4,)) if olds else pltpu.SemaphoreType.DMA,
            pltpu.SemaphoreType.DMA((QUARTERS,)),
            pltpu.SemaphoreType.DMA((2 * QUARTERS,)),
        ],
        compiler_params=pltpu.CompilerParams(vmem_limit_bytes=limit),
        cost_estimate=pl.CostEstimate(
            flops=25 * STEPS * tall * points * lanes, bytes_accessed=12 * tall * points * lanes,
            transcendentals=0,
        ),
        name=name,
    )(facts, *inputs, *olds)


def inner_steps(facts, start):
    rows, points, lanes = start.shape
    part = (rows - 2 * STEPS) // QUARTERS * points + META
    inputs = [start.reshape(-1, lanes)]
    return step_call(
        inner_kernel, "inner_steps", facts, inputs, [], rows, points, rows, QUARTERS * part, part,
        INNER_LIMIT,
    )


def outer_steps(facts, start, before, after, stepped):
    rows, points, lanes = start.shape
    inputs = [v.reshape(-1, lanes) for v in (start, before, after)]
    return step_call(
        outer_kernel, "outer_steps", facts, inputs, [stepped], rows, points, 6 * STEPS,
        2 * QUARTERS * points, 2 * points, OUTER_LIMIT,
    )


def combine_kernel(grids, edge, table_ref, *refs):
    inner, outer = refs[:QUARTERS], refs[QUARTERS:-2]
    half = inner[0].shape[0] // 2 // SUB * SUB
    lanes = inner[0].shape[1]
    mine = jnp.bitwise_and(shifted_place(), 1)
    total = None
    for index in range(QUARTERS):
        head = inner[index]
        triple = jnp.max(head[2 * half : 2 * half + 1, :]).astype(jnp.int32)
        scale = jnp.max(head[2 * half + 1 : 2 * half + 2, :]) / grids
        columns = []
        for member in (1 - mine, mine):
            begin = pl.multiple_of(member * half, SUB)
            if edge:
                columns.append(head[pl.ds(begin + 2 * SUB, SUB), :])
                columns.append(outer[index][pl.ds(pl.multiple_of(member * SUB, SUB), SUB), :])
            else:
                columns.append(head[pl.ds(begin, SUB), :])
                columns.append(head[pl.ds(begin + SUB, SUB), :])
        wide = jnp.concatenate(columns, axis=1) * scale
        stack = jnp.concatenate(split_three(wide), axis=0)
        matrix = table_ref[jnp.clip(triple, 0, len(TRIPLES) - 1)]
        term = jnp.dot(matrix, stack, preferred_element_type=jnp.float32)
        total = term if total is None else total + term
    for side, out_ref in enumerate(refs[-2:]):
        for row in range(2):
            begin = (2 * side + row) * lanes
            out_ref[row] = total[:, begin : begin + lanes]


def combine(table, inner, outer, grids):
    lanes = inner[0].shape[1]
    shape = jax.ShapeDtypeStruct((2, COUNT, lanes), jnp.float32)
    return pl.pallas_call(
        lambda *refs: combine_kernel(grids, bool(outer), *refs),
        out_shape=[shape, shape],
        compiler_params=pltpu.CompilerParams(vmem_limit_bytes=24 * 2**20),
        cost_estimate=pl.CostEstimate(
            flops=2 * QUARTERS * 3 * SUB * COUNT * 4 * lanes, bytes_accessed=2**20, transcendentals=0
        ),
        name="combine",
    )(table, *inner, *outer)


def fill_kernel(chunks, width, with_base, where_ref, matrix_ref, *refs):
    sources = refs[:chunks]
    out_ref, scratch, sems = refs[chunks + with_base :]
    square = MLEN**2
    copies = []
    for index, source in enumerate(sources):
        lanes = source.shape[2]
        parts = split_three(jnp.concatenate([source[row] for row in range(width)], axis=1))
        level = {}
        begin = 0
        for (low, high), members in GROUPS:
            block = matrix_ref[begin : begin + square * len(members), : 3 * (high - low)]
            stack = jnp.concatenate([part[low:high] for part in parts], axis=0)
            result = jnp.dot(block, stack, preferred_element_type=jnp.float32)
            for k, member in enumerate(members):
                level[member] = result[k * square : (k + 1) * square]
            begin += square * len(members)
        nodal = dict(level)
        nodal[4] = level[4] + 0.5 * nodal[0]
        nodal[2] = level[2] + 0.5 * (nodal[0] + nodal[4])
        nodal[6] = level[6] + 0.5 * nodal[4]
        for odd in (1, 3, 5):
            nodal[odd] = level[odd] + 0.5 * (nodal[odd - 1] + nodal[odd + 1])
        nodal[7] = level[7] + 0.5 * nodal[6]
        for row in range(width):
            for c in range(MLEN):
                scratch[index * width + row, c * square : (c + 1) * square, :] = nodal[c][
                    :, row * lanes : (row + 1) * lanes
                ]
        for row in range(width):
            copy = pltpu.make_async_copy(
                scratch.at[index * width + row],
                out_ref.at[where_ref[index * width + row]],
                sems.at[index * width + row],
            )
            copy.start()
            copies.append(copy)
    for copy in copies:
        copy.wait()


def fill(where, matrix, sources, rows, base):
    width, _, lanes = sources[0].shape
    chunks = len(sources)
    with_base = 0 if base is None else 1
    args = [where, matrix, *sources] + ([base] if with_base else [])
    anywhere = pl.BlockSpec(memory_space=pl.ANY)
    vector = pl.BlockSpec(memory_space=pltpu.VMEM)
    return pl.pallas_call(
        lambda *refs: fill_kernel(chunks, width, with_base, *refs),
        out_shape=jax.ShapeDtypeStruct((rows, MLEN**3, lanes), jnp.float32),
        in_specs=[pl.BlockSpec(memory_space=pltpu.SMEM)] + [vector] * (1 + chunks) + [anywhere] * with_base,
        out_specs=anywhere,
        input_output_aliases={2 + chunks: 0} if with_base else {},
        scratch_shapes=[
            pltpu.VMEM((chunks * width, MLEN**3, lanes), jnp.float32),
            pltpu.SemaphoreType.DMA((chunks * width,)),
        ],
        compiler_params=pltpu.CompilerParams(vmem_limit_bytes=24 * 2**20),
        cost_estimate=pl.CostEstimate(
            flops=6 * chunks * width * matrix.size * lanes,
            bytes_accessed=4 * chunks * width * (MLEN**3 + COUNT) * lanes,
            transcendentals=0,
        ),
        name="fill",
    )(*args)


def per_device(initial, diffusion, drift, levels, weights):
    values = initial[0]
    rows, points, _ = values.shape
    dom_size = lax.axis_size("dom")
    grid_size = lax.axis_size("grid")
    columns = grid_size // ZLEN
    place = shifted_place()

    def swap(v, bits):
        pairs = []
        for grid in range(grid_size):
            z, y = divmod(grid, columns)
            for dom in range(dom_size):
                core = dom % 2
                partner = (((z - core) % ZLEN ^ bits) + core) % ZLEN * columns + y
                pairs.append((grid * dom_size + dom, partner * dom_size + dom))
        return lax.ppermute(v, ("grid", "dom"), pairs)

    across = lambda v: lax.ppermute(v, "grid", [(i, i ^ 1) for i in range(grid_size)])

    up = [(i, i + 1) for i in range(dom_size - 1)]
    down = [(j, i) for i, j in up]
    before = lax.ppermute(values[rows - STEPS :], "dom", up)
    after = lax.ppermute(values[:STEPS], "dom", down)
    numbers = [levels[0].astype(jnp.float32), weights.astype(jnp.float32), diffusion[0], drift[0]]
    facts = jnp.concatenate(numbers)
    stepped, *inner = inner_steps(facts, values)
    inner = [inner[0]] + [swap(inner[k], 2 * k) for k in ORDER]
    stepped, *outer = outer_steps(facts, values, before, after, stepped)
    held = lax.optimization_barrier((*inner, *outer))
    inner, outer = held[:QUARTERS], held[QUARTERS:]
    outer = [outer[0]] + [swap(outer[k], 2 * k) for k in ORDER]
    stepped = stepped.reshape(rows, points, -1)

    table = jnp.asarray(placing_table(), jnp.bfloat16)
    sums = []
    for pieces in ([], outer):
        theirs, mine = combine(table, inner, pieces, grid_size)
        partial = mine + swap(theirs, 1)
        sums.append(partial + across(partial))

    plus = [(i, (i + columns) % grid_size) for i in range(grid_size)]
    minus = [(j, i) for i, j in plus]
    matrix = jnp.asarray(fill_matrix(), jnp.bfloat16)

    def spots(source, edge):
        source = jnp.bitwise_and(source + ZLEN, ZLEN - 1)
        begin = STEPS + 3 * source
        if not edge:
            return [begin, begin + 1]
        side = jnp.bitwise_and(source, 1) * (rows - STEPS)
        return [begin + 2, side + jnp.right_shift(source, 1)]

    ups, downs = list(sums), list(sums)
    chunks = list(sums)
    where = spots(place, 0) + spots(place, 1)
    for hop in range(1, ZLEN // 2):
        for s in range(2):
            next_up = lax.ppermute(ups[s], "grid", plus)
            next_down = lax.ppermute(downs[s], "grid", minus)
            ups[s], downs[s] = next_up, next_down
            chunks += [next_up, next_down]
            where += spots(place - hop, s) + spots(place + hop, s)
    last = [lax.ppermute(ups[0], "grid", plus), lax.ppermute(downs[1], "grid", minus)]
    combined = fill(jnp.stack(where), matrix, chunks, rows, None)
    last, combined = lax.optimization_barrier((last, combined))
    spot = spots(place + ZLEN // 2, 0) + spots(place + ZLEN // 2, 1)
    combined = fill(jnp.stack(spot), matrix, last, rows, combined)
    return stepped[None], combined.reshape(rows, MLEN, MLEN, MLEN, -1)


def solution(mesh):
    in_specs = (
        P("grid", "dom", None, None),
        P("grid", None),
        P("grid", None),
        P("grid", None),
        P("grid"),
    )
    out_specs = (P("grid", "dom", None, None), P("dom", None, None, None, None))
    return jax.shard_map(
        per_device, mesh=mesh, in_specs=in_specs, out_specs=out_specs, check_vma=False
    )
```

```python
import itertools

import jax
import jax.numpy as jnp
import numpy as np
from jax import lax
from jax.experimental import pallas as pl
from jax.experimental.pallas import tpu as pltpu
from jax.sharding import PartitionSpec as P

STEPS = 4
MLEN = 8
FINEST = 3
LEVEL_SUM = 6
ZLEN = 8
QUARTERS = 4
ORDER = (2, 1, 3)
INNER_LIMIT = 24 * 2**20
OUTER_LIMIT = 24 * 2**20


def rank_of(coordinate):
    if coordinate % 4 == 0:
        return 1
    return 2 if coordinate % 2 == 0 else 3


def union_points():
    points = []
    for first in (0, 4, 2, 6, 1, 3, 5, 7):
        for second, third in itertools.product(range(MLEN), repeat=2):
            if rank_of(first) + rank_of(second) + rank_of(third) <= LEVEL_SUM:
                points.append((first, second, third))
    return np.array(points, np.int32)


POINTS = union_points()
COUNT = len(POINTS)
SUB = 64
META = 8
TRIPLES = ((1, 2), (1, 3), (2, 1), (2, 2), (2, 3), (3, 1), (3, 2))
GROUPS = (((0, 48), (0,)), ((48, 96), (4,)), ((96, 160), (2, 6)), ((160, 208), (1, 3, 5, 7)))


def nodal_matrix(length_dim):
    matrix = np.eye(length_dim)
    stride = length_dim // 2
    while stride >= 1:
        for position in range(stride, length_dim, 2 * stride):
            matrix[position] = matrix[position] + 0.5 * matrix[position - stride]
            if position + stride < length_dim:
                matrix[position] = matrix[position] + 0.5 * matrix[position + stride]
        stride = stride // 2
    return matrix


def fill_matrix():
    nodal = nodal_matrix(MLEN)
    square = MLEN**2
    matrix = np.zeros((MLEN, MLEN, MLEN, COUNT))
    for column, (first, second, third) in enumerate(POINTS):
        matrix[first, :, :, column] = np.outer(nodal[:, second], nodal[:, third])
    matrix = matrix.reshape(MLEN, square, COUNT)
    packed = np.zeros((MLEN * square, 256))
    begin = 0
    for (low, high), members in GROUPS:
        block = matrix[list(members), :, low:high].reshape(-1, high - low)
        packed[begin : begin + len(block), : 3 * (high - low)] = np.tile(block, (1, 3))
        begin += len(block)
    return packed

def placing_table():
    tables = []
    for first, second in TRIPLES:
        level = (first, second, LEVEL_SUM - first - second)
        length = [2**v for v in level]
        surplus = np.ones((1, 1))
        for n in length:
            surplus = np.kron(surplus, np.round(2.0 * np.linalg.inv(nodal_matrix(n))) / 2.0)
        target = np.zeros((COUNT, SUB))
        for column, coords in enumerate(itertools.product(*[range(n) for n in length])):
            point = [c * (MLEN // n) for c, n in zip(coords, length)]
            target[np.all(POINTS == point, axis=1), column] = 1.0
        tables.append(np.tile(target @ surplus, (1, 3)))
    return np.stack(tables)


def split_three(values):
    high = values.astype(jnp.bfloat16)
    rest = values - high.astype(jnp.float32)
    middle = rest.astype(jnp.bfloat16)
    low = (rest - middle.astype(jnp.float32)).astype(jnp.bfloat16)
    return high, middle, low


class Stencil:
    def __init__(self, points, facts_ref, coef_ref):
        self.points, self.coef_ref = points, coef_ref
        levels = [facts_ref[dim].astype(jnp.int32) for dim in range(3)]
        spread = [facts_ref[4 + dim] for dim in range(5)]
        drift = [0.5 * facts_ref[9 + dim] for dim in range(5)]
        place = lax.broadcasted_iota(jnp.int32, (points, 128), 0)
        lane = lax.broadcasted_iota(jnp.int32, (8, 128), 1)
        sublane = lax.broadcasted_iota(jnp.int32, (META, 128), 0)
        offsets = [levels[1] + levels[2], levels[2], jnp.int32(0)]
        self.strides = []
        self.centre_rate = 1.0 - 2.0 * spread[0] - 2.0 * spread[4]
        for dim in range(3):
            length = jnp.left_shift(jnp.int32(1), levels[dim])
            coord = jnp.bitwise_and(jnp.right_shift(place, offsets[dim]), length - 1)
            rise, fall = spread[dim + 1] + drift[dim + 1], spread[dim + 1] - drift[dim + 1]
            coef_ref[2 * dim] = jnp.where(coord < length - 1, rise, 0.0)
            coef_ref[2 * dim + 1] = jnp.where(coord > 0, fall, 0.0)
            self.strides.append(jnp.left_shift(jnp.int32(1), offsets[dim]))
            self.centre_rate = self.centre_rate - 2.0 * spread[dim + 1]
        self.row_up, self.row_down = spread[0] + drift[0], spread[0] - drift[0]
        self.lane_up = jnp.where(lane < 127, spread[4] + drift[4], 0.0)
        self.lane_down = jnp.where(lane > 0, spread[4] - drift[4], 0.0)
        triple = (3 * levels[0] + levels[1] - 5).astype(jnp.float32)
        self.head = jnp.where(sublane == 0, triple, facts_ref[3])

    def advance(self, source, target, spans, locate, mask):
        points = self.points

        def tile(tile_index, carry):
            base = pl.multiple_of(tile_index * 8, 8)
            coefs = [self.coef_ref[i, pl.ds(base, 8), :] for i in range(6)]

            def at(row):
                return source[pl.ds(pl.multiple_of(row * points + base, 8), 8), :]

            for low, high in spans:
                below, centre = at(low - 1), at(low)
                for row in range(low, high):
                    above = at(row + 1)
                    offset = row * points + base
                    total = centre * self.centre_rate + above * self.row_up + below * self.row_down
                    total = total + pltpu.roll(centre, 127, 1) * self.lane_up
                    total = total + pltpu.roll(centre, 1, 1) * self.lane_down
                    for dim in range(3):
                        stride = self.strides[dim]
                        total = total + source[pl.ds(offset + stride, 8), :] * coefs[2 * dim]
                        total = total + source[pl.ds(offset - stride, 8), :] * coefs[2 * dim + 1]
                    total = mask(row, total)
                    target[pl.ds(pl.multiple_of(locate(row) + base, 8), 8), :] = total
                    below, centre = centre, above
            return carry

        lax.fori_loop(0, points // 8, tile, 0, unroll=4)


def shifted_place():
    columns = lax.axis_size("grid") // ZLEN
    core = jnp.bitwise_and(lax.axis_index("dom"), 1)
    return jnp.bitwise_and(lax.axis_index("grid") // columns - core + ZLEN, ZLEN - 1)


def inner_kernel(rows, points, facts_ref, start_ref, stepped_ref, *rest):
    parts = rest[:QUARTERS]
    first, second, final, coef_ref, load_sem, part_sem, store_sem = rest[QUARTERS:]
    share = (rows - 2 * STEPS) // QUARTERS
    size = share * points
    block = size + META
    load = pltpu.make_async_copy(start_ref, first, load_sem)
    load.start()
    quarter = jnp.right_shift(shifted_place(), 1)
    stencil = Stencil(points, facts_ref, coef_ref)
    for index in range(QUARTERS):
        final[index * block + size : (index + 1) * block, :] = stencil.head
    load.wait()

    def located(row):
        group, inner = divmod(row - STEPS, share)
        return group * block + inner * points

    same = lambda row: row * points
    keep = lambda row, value: value
    buffers = [first, second, first, second, final]
    for step in range(1, STEPS + 1):
        place = located if step == STEPS else same
        stencil.advance(buffers[step - 1], buffers[step], [(step, rows - step)], place, keep)

    copies = []
    for index, part in enumerate(parts):
        begin = pl.multiple_of(jnp.bitwise_xor(quarter, index) * block, 8)
        copies.append(
            pltpu.make_async_copy(final.at[pl.ds(begin, block)], part, part_sem.at[index])
        )
    for index in range(QUARTERS):
        copies.append(
            pltpu.make_async_copy(
                final.at[pl.ds(index * block, size)],
                stepped_ref.at[pl.ds(STEPS * points + index * size, size)],
                store_sem.at[index],
            )
        )
    for copy in copies:
        copy.start()
    for copy in copies:
        copy.wait()


def outer_kernel(rows, points, facts_ref, start_ref, before_ref, after_ref, _, stepped_ref, *rest):
    parts = rest[:QUARTERS]
    first, second, final, coef_ref, load_sem, part_sem, store_sem = rest[QUARTERS:]
    halo, near = STEPS * points, 2 * STEPS * points
    sides = [
        (before_ref, 0, halo),
        (start_ref.at[pl.ds(0, near)], halo, near),
        (start_ref.at[pl.ds(rows * points - near, near)], halo + near, near),
        (after_ref, halo + 2 * near, halo),
    ]
    loads = [
        pltpu.make_async_copy(source, first.at[pl.ds(begin, size)], load_sem.at[i])
        for i, (source, begin, size) in enumerate(sides)
    ]
    for load in loads:
        load.start()
    quarter = jnp.right_shift(shifted_place(), 1)
    dom = lax.axis_index("dom")
    keep_low = (dom > 0).astype(jnp.float32)
    keep_high = (dom < lax.axis_size("dom") - 1).astype(jnp.float32)
    stencil = Stencil(points, facts_ref, coef_ref)
    for load in loads:
        load.wait()

    strip = 3 * STEPS

    def mask(row, value):
        if row < STEPS:
            return value * keep_low
        if row >= 2 * strip - STEPS:
            return value * keep_high
        return value

    def located(row):
        side, inner = divmod(row, strip)
        return (2 * (inner - STEPS) + side) * points

    same = lambda row: row * points
    buffers = [first, second, first, second, final]
    for step in range(1, STEPS + 1):
        place = located if step == STEPS else same
        spans = [(step, strip - step), (strip + step, 2 * strip - step)]
        stencil.advance(buffers[step - 1], buffers[step], spans, place, mask)

    copies = []
    for index, part in enumerate(parts):
        begin = pl.multiple_of(jnp.bitwise_xor(quarter, index) * (2 * points), 8)
        copies.append(
            pltpu.make_async_copy(final.at[pl.ds(begin, 2 * points)], part, part_sem.at[index])
        )
    for index in range(2 * QUARTERS):
        row = index // 2 + index % 2 * (rows - STEPS)
        copies.append(
            pltpu.make_async_copy(
                final.at[pl.ds(index * points, points)],
                stepped_ref.at[pl.ds(row * points, points)],
                store_sem.at[index],
            )
        )
    for copy in copies:
        copy.start()
    for copy in copies:
        copy.wait()


def step_call(kernel, name, facts, inputs, olds, rows, points, tall, wide, part, limit):
    lanes = inputs[0].shape[-1]
    anywhere = pl.BlockSpec(memory_space=pl.ANY)
    buffer = pltpu.VMEM((tall * points, lanes), jnp.float32)
    return pl.pallas_call(
        lambda *refs: kernel(rows, points, *refs),
        out_shape=[jax.ShapeDtypeStruct((rows * points, lanes), jnp.float32)]
        + [jax.ShapeDtypeStruct((part, lanes), jnp.float32)] * QUARTERS,
        in_specs=[pl.BlockSpec(memory_space=pltpu.SMEM)] + [anywhere] * (len(inputs) + len(olds)),
        out_specs=[anywhere] * (1 + QUARTERS),
        input_output_aliases={1 + len(inputs): 0} if olds else {},
        scratch_shapes=[
            buffer,
            buffer,
            pltpu.VMEM((wide, lanes), jnp.float32),
            pltpu.VMEM((6, points, lanes), jnp.float32),
            pltpu.SemaphoreType.DMA((4,)) if olds else pltpu.SemaphoreType.DMA,
            pltpu.SemaphoreType.DMA((QUARTERS,)),
            pltpu.SemaphoreType.DMA((2 * QUARTERS,)),
        ],
        compiler_params=pltpu.CompilerParams(vmem_limit_bytes=limit),
        cost_estimate=pl.CostEstimate(
            flops=25 * STEPS * tall * points * lanes, bytes_accessed=12 * tall * points * lanes,
            transcendentals=0,
        ),
        name=name,
    )(facts, *inputs, *olds)


def inner_steps(facts, start):
    rows, points, lanes = start.shape
    part = (rows - 2 * STEPS) // QUARTERS * points + META
    inputs = [start.reshape(-1, lanes)]
    return step_call(
        inner_kernel, "inner_steps", facts, inputs, [], rows, points, rows, QUARTERS * part, part,
        INNER_LIMIT,
    )


def outer_steps(facts, start, before, after, stepped):
    rows, points, lanes = start.shape
    inputs = [v.reshape(-1, lanes) for v in (start, before, after)]
    return step_call(
        outer_kernel, "outer_steps", facts, inputs, [stepped], rows, points, 6 * STEPS,
        2 * QUARTERS * points, 2 * points, OUTER_LIMIT,
    )


def combine_kernel(grids, edge, table_ref, *refs):
    inner, outer = refs[:QUARTERS], refs[QUARTERS:-2] if edge else []
    outs = refs[-2:] if edge else refs[QUARTERS : QUARTERS + 2]
    half = inner[0].shape[0] // 2 // SUB * SUB
    lanes = inner[0].shape[1]
    mine = jnp.bitwise_and(shifted_place(), 1)
    total = None
    for index in range(QUARTERS):
        head = inner[index]
        triple = jnp.max(head[2 * half : 2 * half + 1, :]).astype(jnp.int32)
        scale = jnp.max(head[2 * half + 1 : 2 * half + 2, :]) / grids
        columns = []
        for member in (1 - mine, mine):
            begin = pl.multiple_of(member * half, SUB)
            if edge:
                columns.append(head[pl.ds(begin + 2 * SUB, SUB), :])
                columns.append(outer[index][pl.ds(pl.multiple_of(member * SUB, SUB), SUB), :])
            else:
                columns.append(head[pl.ds(begin, SUB), :])
                columns.append(head[pl.ds(begin + SUB, SUB), :])
        wide = jnp.concatenate(columns, axis=1) * scale
        stack = jnp.concatenate(split_three(wide), axis=0)
        if edge:
            matrix = table_ref[index]
        else:
            matrix = table_ref[jnp.clip(triple, 0, len(TRIPLES) - 1)]
            refs[-1][index] = matrix
        term = jnp.dot(matrix, stack, preferred_element_type=jnp.float32)
        total = term if total is None else total + term
    for side, out_ref in enumerate(outs):
        for row in range(2):
            begin = (2 * side + row) * lanes
            out_ref[row] = total[:, begin : begin + lanes]


def combine(table, inner, outer, grids):
    lanes = inner[0].shape[1]
    shape = jax.ShapeDtypeStruct((2, COUNT, lanes), jnp.float32)
    chosen = jax.ShapeDtypeStruct((QUARTERS, *table.shape[1:]), table.dtype)
    return pl.pallas_call(
        lambda *refs: combine_kernel(grids, bool(outer), *refs),
        out_shape=[shape, shape] + ([] if outer else [chosen]),
        compiler_params=pltpu.CompilerParams(vmem_limit_bytes=24 * 2**20),
        cost_estimate=pl.CostEstimate(
            flops=2 * QUARTERS * 3 * SUB * COUNT * 4 * lanes, bytes_accessed=2**20, transcendentals=0
        ),
        name="combine",
    )(table, *inner, *outer)


def fill_kernel(chunks, width, with_base, where_ref, matrix_ref, *refs):
    sources = refs[:chunks]
    out_ref, scratch, sems = refs[chunks + with_base :]
    square = MLEN**2
    copies = []
    for index, source in enumerate(sources):
        lanes = source.shape[2]
        parts = split_three(jnp.concatenate([source[row] for row in range(width)], axis=1))
        level = {}
        begin = 0
        for (low, high), members in GROUPS:
            block = matrix_ref[begin : begin + square * len(members), : 3 * (high - low)]
            stack = jnp.concatenate([part[low:high] for part in parts], axis=0)
            result = jnp.dot(block, stack, preferred_element_type=jnp.float32)
            for k, member in enumerate(members):
                level[member] = result[k * square : (k + 1) * square]
            begin += square * len(members)
        nodal = dict(level)
        nodal[4] = level[4] + 0.5 * nodal[0]
        nodal[2] = level[2] + 0.5 * (nodal[0] + nodal[4])
        nodal[6] = level[6] + 0.5 * nodal[4]
        for odd in (1, 3, 5):
            nodal[odd] = level[odd] + 0.5 * (nodal[odd - 1] + nodal[odd + 1])
        nodal[7] = level[7] + 0.5 * nodal[6]
        for row in range(width):
            for c in range(MLEN):
                scratch[index * width + row, c * square : (c + 1) * square, :] = nodal[c][
                    :, row * lanes : (row + 1) * lanes
                ]
        for row in range(width):
            copy = pltpu.make_async_copy(
                scratch.at[index * width + row],
                out_ref.at[where_ref[index * width + row]],
                sems.at[index * width + row],
            )
            copy.start()
            copies.append(copy)
    for copy in copies:
        copy.wait()


def fill(where, matrix, sources, rows, base):
    width, _, lanes = sources[0].shape
    chunks = len(sources)
    with_base = 0 if base is None else 1
    args = [where, matrix, *sources] + ([base] if with_base else [])
    anywhere = pl.BlockSpec(memory_space=pl.ANY)
    vector = pl.BlockSpec(memory_space=pltpu.VMEM)
    return pl.pallas_call(
        lambda *refs: fill_kernel(chunks, width, with_base, *refs),
        out_shape=jax.ShapeDtypeStruct((rows, MLEN**3, lanes), jnp.float32),
        in_specs=[pl.BlockSpec(memory_space=pltpu.SMEM)] + [vector] * (1 + chunks) + [anywhere] * with_base,
        out_specs=anywhere,
        input_output_aliases={2 + chunks: 0} if with_base else {},
        scratch_shapes=[
            pltpu.VMEM((chunks * width, MLEN**3, lanes), jnp.float32),
            pltpu.SemaphoreType.DMA((chunks * width,)),
        ],
        compiler_params=pltpu.CompilerParams(vmem_limit_bytes=24 * 2**20),
        cost_estimate=pl.CostEstimate(
            flops=6 * chunks * width * matrix.size * lanes,
            bytes_accessed=4 * chunks * width * (MLEN**3 + COUNT) * lanes,
            transcendentals=0,
        ),
        name="fill",
    )(*args)


def per_device(initial, diffusion, drift, levels, weights):
    values = initial[0]
    rows, points, _ = values.shape
    dom_size = lax.axis_size("dom")
    grid_size = lax.axis_size("grid")
    columns = grid_size // ZLEN
    place = shifted_place()

    def swap(v, bits, offset=0):
        pairs = []
        for grid in range(grid_size):
            z, y = divmod(grid, columns)
            for dom in range(dom_size):
                origin = dom % 2 + offset
                partner = (((z - origin) % ZLEN ^ bits) + origin) % ZLEN * columns + y
                pairs.append((grid * dom_size + dom, partner * dom_size + dom))
        return lax.ppermute(v, ("grid", "dom"), pairs)

    across = lambda v: lax.ppermute(v, "grid", [(i, i ^ 1) for i in range(grid_size)])

    up = [(i, i + 1) for i in range(dom_size - 1)]
    down = [(j, i) for i, j in up]
    before = lax.ppermute(values[rows - STEPS :], "dom", up)
    after = lax.ppermute(values[:STEPS], "dom", down)
    numbers = [levels[0].astype(jnp.float32), weights.astype(jnp.float32), diffusion[0], drift[0]]
    facts = jnp.concatenate(numbers)
    stepped, *inner = inner_steps(facts, values)
    inner = [inner[0]] + [swap(inner[k], 2 * k) for k in ORDER]
    stepped, *outer = outer_steps(facts, values, before, after, stepped)
    outer = [outer[0]] + [swap(outer[k], 2 * k) for k in ORDER]
    stepped = stepped.reshape(rows, points, -1)

    table = jnp.asarray(placing_table(), jnp.bfloat16)
    sums = []
    for pieces in ([], outer):
        theirs, mine, *rest = combine(table, inner, pieces, grid_size)
        table = rest[0] if rest else None
        partial = mine + swap(theirs, 1)
        sums.append(partial + across(partial))

    ring_sign = 1 - 2 * jnp.bitwise_and(place, 1)
    matrix = jnp.asarray(fill_matrix(), jnp.bfloat16)

    def spots(source, edge):
        source = jnp.bitwise_and(source + ZLEN, ZLEN - 1)
        begin = STEPS + 3 * source
        if not edge:
            return [begin, begin + 1]
        side = jnp.bitwise_and(source, 1) * (rows - STEPS)
        return [begin + 2, side + jnp.right_shift(source, 1)]

    ups, downs = list(sums), list(sums)
    chunks = list(sums)
    where = spots(place, 0) + spots(place, 1)
    for hop in range(1, ZLEN // 2):
        for s in range(2):
            next_up = swap(downs[s], 1)
            next_down = swap(ups[s], 1, 1)
            ups[s], downs[s] = next_up, next_down
            chunks += [next_up, next_down]
            where += spots(place + hop * ring_sign, s) + spots(place - hop * ring_sign, s)
    last = [swap(downs[0], 1), swap(ups[1], 1, 1)]
    combined = fill(jnp.stack(where), matrix, chunks, rows, None)
    last, combined = lax.optimization_barrier((last, combined))
    spot = spots(place + ZLEN // 2, 0) + spots(place + ZLEN // 2, 1)
    combined = fill(jnp.stack(spot), matrix, last, rows, combined)
    return stepped[None], combined.reshape(rows, MLEN, MLEN, MLEN, -1)


def solution(mesh):
    in_specs = (
        P("grid", "dom", None, None),
        P("grid", None),
        P("grid", None),
        P("grid", None),
        P("grid"),
    )
    out_specs = (P("grid", "dom", None, None), P("dom", None, None, None, None))
    return jax.shard_map(
        per_device, mesh=mesh, in_specs=in_specs, out_specs=out_specs, check_vma=False
    )
```

```python
import itertools

import jax
import jax.numpy as jnp
import numpy as np
from jax import lax
from jax.experimental import pallas as pl
from jax.experimental.pallas import tpu as pltpu
from jax.sharding import PartitionSpec as P

STEPS = 4
MLEN = 8
FINEST = 3
LEVEL_SUM = 6
ZLEN = 8
QUARTERS = 4
ORDER = (2, 1, 3)
INNER_LIMIT = 24 * 2**20
OUTER_LIMIT = 24 * 2**20


def rank_of(coordinate):
    if coordinate % 4 == 0:
        return 1
    return 2 if coordinate % 2 == 0 else 3


def union_points():
    points = []
    for first in (0, 4, 2, 6, 1, 3, 5, 7):
        for second, third in itertools.product(range(MLEN), repeat=2):
            if rank_of(first) + rank_of(second) + rank_of(third) <= LEVEL_SUM:
                points.append((first, second, third))
    return np.array(points, np.int32)


POINTS = union_points()
COUNT = len(POINTS)
SUB = 64
META = 8
TRIPLES = ((1, 2), (1, 3), (2, 1), (2, 2), (2, 3), (3, 1), (3, 2))
GROUPS = (((0, 48), (0,)), ((48, 96), (4,)), ((96, 160), (2, 6)), ((160, 208), (1, 3, 5, 7)))


def nodal_matrix(length_dim):
    matrix = np.eye(length_dim)
    stride = length_dim // 2
    while stride >= 1:
        for position in range(stride, length_dim, 2 * stride):
            matrix[position] = matrix[position] + 0.5 * matrix[position - stride]
            if position + stride < length_dim:
                matrix[position] = matrix[position] + 0.5 * matrix[position + stride]
        stride = stride // 2
    return matrix


def fill_matrix():
    nodal = nodal_matrix(MLEN)
    square = MLEN**2
    matrix = np.zeros((MLEN, MLEN, MLEN, COUNT))
    for column, (first, second, third) in enumerate(POINTS):
        matrix[first, :, :, column] = np.outer(nodal[:, second], nodal[:, third])
    matrix = matrix.reshape(MLEN, square, COUNT)
    packed = np.zeros((MLEN * square, 256))
    begin = 0
    for (low, high), members in GROUPS:
        block = matrix[list(members), :, low:high].reshape(-1, high - low)
        packed[begin : begin + len(block), : 3 * (high - low)] = np.tile(block, (1, 3))
        begin += len(block)
    return packed

def placing_table():
    tables = []
    for first, second in TRIPLES:
        level = (first, second, LEVEL_SUM - first - second)
        length = [2**v for v in level]
        surplus = np.ones((1, 1))
        for n in length:
            surplus = np.kron(surplus, np.round(2.0 * np.linalg.inv(nodal_matrix(n))) / 2.0)
        target = np.zeros((COUNT, SUB))
        for column, coords in enumerate(itertools.product(*[range(n) for n in length])):
            point = [c * (MLEN // n) for c, n in zip(coords, length)]
            target[np.all(POINTS == point, axis=1), column] = 1.0
        tables.append(np.tile(target @ surplus, (1, 3)))
    return np.stack(tables)


def split_three(values):
    high = values.astype(jnp.bfloat16)
    rest = values - high.astype(jnp.float32)
    middle = rest.astype(jnp.bfloat16)
    low = (rest - middle.astype(jnp.float32)).astype(jnp.bfloat16)
    return high, middle, low


class Stencil:
    def __init__(self, points, facts_ref, coef_ref):
        self.points, self.coef_ref = points, coef_ref
        levels = [facts_ref[dim].astype(jnp.int32) for dim in range(3)]
        spread = [facts_ref[4 + dim] for dim in range(5)]
        drift = [0.5 * facts_ref[9 + dim] for dim in range(5)]
        place = lax.broadcasted_iota(jnp.int32, (points, 128), 0)
        lane = lax.broadcasted_iota(jnp.int32, (8, 128), 1)
        sublane = lax.broadcasted_iota(jnp.int32, (META, 128), 0)
        offsets = [levels[1] + levels[2], levels[2], jnp.int32(0)]
        self.strides = []
        self.centre_rate = 1.0 - 2.0 * spread[0] - 2.0 * spread[4]
        for dim in range(3):
            length = jnp.left_shift(jnp.int32(1), levels[dim])
            coord = jnp.bitwise_and(jnp.right_shift(place, offsets[dim]), length - 1)
            rise, fall = spread[dim + 1] + drift[dim + 1], spread[dim + 1] - drift[dim + 1]
            coef_ref[2 * dim] = jnp.where(coord < length - 1, rise, 0.0)
            coef_ref[2 * dim + 1] = jnp.where(coord > 0, fall, 0.0)
            self.strides.append(jnp.left_shift(jnp.int32(1), offsets[dim]))
            self.centre_rate = self.centre_rate - 2.0 * spread[dim + 1]
        self.row_up, self.row_down = spread[0] + drift[0], spread[0] - drift[0]
        self.lane_up = jnp.where(lane < 127, spread[4] + drift[4], 0.0)
        self.lane_down = jnp.where(lane > 0, spread[4] - drift[4], 0.0)
        triple = (3 * levels[0] + levels[1] - 5).astype(jnp.float32)
        self.head = jnp.where(sublane == 0, triple, facts_ref[3])

    def advance(self, source, target, spans, locate, mask):
        points = self.points

        def tile(tile_index, carry):
            base = pl.multiple_of(tile_index * 8, 8)
            coefs = [self.coef_ref[i, pl.ds(base, 8), :] for i in range(6)]

            def at(row):
                return source[pl.ds(pl.multiple_of(row * points + base, 8), 8), :]

            for low, high in spans:
                below, centre = at(low - 1), at(low)
                for row in range(low, high):
                    above = at(row + 1)
                    offset = row * points + base
                    total = centre * self.centre_rate + above * self.row_up + below * self.row_down
                    total = total + pltpu.roll(centre, 127, 1) * self.lane_up
                    total = total + pltpu.roll(centre, 1, 1) * self.lane_down
                    for dim in range(3):
                        stride = self.strides[dim]
                        total = total + source[pl.ds(offset + stride, 8), :] * coefs[2 * dim]
                        total = total + source[pl.ds(offset - stride, 8), :] * coefs[2 * dim + 1]
                    total = mask(row, total)
                    target[pl.ds(pl.multiple_of(locate(row) + base, 8), 8), :] = total
                    below, centre = centre, above
            return carry

        lax.fori_loop(0, points // 8, tile, 0, unroll=4)


def shifted_place():
    columns = lax.axis_size("grid") // ZLEN
    core = jnp.bitwise_and(lax.axis_index("dom"), 1)
    return jnp.bitwise_and(lax.axis_index("grid") // columns - core + ZLEN, ZLEN - 1)


def inner_kernel(rows, points, facts_ref, start_ref, stepped_ref, *rest):
    parts, edges = rest[:QUARTERS], rest[QUARTERS : QUARTERS + 3]
    first, second, final, coef_ref, load_sem, part_sem, store_sem = rest[QUARTERS + 3 :]
    share = (rows - 2 * STEPS) // QUARTERS
    size = share * points
    block = size + META
    load = pltpu.make_async_copy(start_ref, first, load_sem)
    load.start()
    quarter = jnp.right_shift(shifted_place(), 1)
    stencil = Stencil(points, facts_ref, coef_ref)
    for index in range(QUARTERS):
        final[index * block + size : (index + 1) * block, :] = stencil.head
    load.wait()
    odd = jnp.bitwise_and(lax.axis_index("dom"), 1)
    halo, near, last = STEPS * points, 2 * STEPS * points, (rows - STEPS) * points
    spans = [
        (pl.multiple_of((1 - odd) * last, 8), halo, edges[0]),
        (pl.multiple_of(odd * last, 8), halo, edges[1]),
        (0, near, edges[2].at[pl.ds(0, near)]),
        (rows * points - near, near, edges[2].at[pl.ds(near, near)]),
    ]
    passed = [
        pltpu.make_async_copy(first.at[pl.ds(begin, size)], target, store_sem.at[QUARTERS + i])
        for i, (begin, size, target) in enumerate(spans)
    ]
    for copy in passed:
        copy.start()

    def located(row):
        group, inner = divmod(row - STEPS, share)
        return group * block + inner * points

    same = lambda row: row * points
    keep = lambda row, value: value
    buffers = [first, second, first, second, final]
    for step in range(1, STEPS + 1):
        place = located if step == STEPS else same
        stencil.advance(buffers[step - 1], buffers[step], [(step, rows - step)], place, keep)
        if step == 1:
            for copy in passed:
                copy.wait()

    copies = []
    for index, part in enumerate(parts):
        begin = pl.multiple_of(jnp.bitwise_xor(quarter, index) * block, 8)
        copies.append(
            pltpu.make_async_copy(final.at[pl.ds(begin, block)], part, part_sem.at[index])
        )
    for index in range(QUARTERS):
        copies.append(
            pltpu.make_async_copy(
                final.at[pl.ds(index * block, size)],
                stepped_ref.at[pl.ds(STEPS * points + index * size, size)],
                store_sem.at[index],
            )
        )
    for copy in copies:
        copy.start()
    for copy in copies:
        copy.wait()


def outer_kernel(rows, points, facts_ref, ends_ref, before_ref, after_ref, _, stepped_ref, *rest):
    parts = rest[:QUARTERS]
    first, second, final, coef_ref, load_sem, part_sem, store_sem = rest[QUARTERS:]
    halo, near = STEPS * points, 2 * STEPS * points
    dom = lax.axis_index("dom")
    near_side = pl.multiple_of((1 - jnp.bitwise_and(dom, 1)) * (halo + 2 * near), 8)
    far_side = pl.multiple_of(jnp.bitwise_and(dom, 1) * (halo + 2 * near), 8)
    sides = [
        (before_ref, near_side, halo),
        (ends_ref, halo, 2 * near),
        (after_ref, far_side, halo),
    ]
    loads = [
        pltpu.make_async_copy(source, first.at[pl.ds(begin, size)], load_sem.at[i])
        for i, (source, begin, size) in enumerate(sides)
    ]
    for load in loads:
        load.start()
    quarter = jnp.right_shift(shifted_place(), 1)
    keep_low = (dom > 0).astype(jnp.float32)
    keep_high = (dom < lax.axis_size("dom") - 1).astype(jnp.float32)
    stencil = Stencil(points, facts_ref, coef_ref)
    for load in loads:
        load.wait()

    strip = 3 * STEPS

    def mask(row, value):
        if row < STEPS:
            return value * keep_low
        if row >= 2 * strip - STEPS:
            return value * keep_high
        return value

    def located(row):
        side, inner = divmod(row, strip)
        return (2 * (inner - STEPS) + side) * points

    same = lambda row: row * points
    buffers = [first, second, first, second, final]
    for step in range(1, STEPS + 1):
        place = located if step == STEPS else same
        spans = [(step, strip - step), (strip + step, 2 * strip - step)]
        stencil.advance(buffers[step - 1], buffers[step], spans, place, mask)

    copies = []
    for index, part in enumerate(parts):
        begin = pl.multiple_of(jnp.bitwise_xor(quarter, index) * (2 * points), 8)
        copies.append(
            pltpu.make_async_copy(final.at[pl.ds(begin, 2 * points)], part, part_sem.at[index])
        )
    for index in range(2 * QUARTERS):
        row = index // 2 + index % 2 * (rows - STEPS)
        copies.append(
            pltpu.make_async_copy(
                final.at[pl.ds(index * points, points)],
                stepped_ref.at[pl.ds(row * points, points)],
                store_sem.at[index],
            )
        )
    for copy in copies:
        copy.start()
    for copy in copies:
        copy.wait()


def step_call(kernel, name, facts, inputs, olds, rows, points, tall, wide, part, extra, limit):
    lanes = inputs[0].shape[-1]
    anywhere = pl.BlockSpec(memory_space=pl.ANY)
    buffer = pltpu.VMEM((tall * points, lanes), jnp.float32)
    return pl.pallas_call(
        lambda *refs: kernel(rows, points, *refs),
        out_shape=[jax.ShapeDtypeStruct((rows * points, lanes), jnp.float32)]
        + [jax.ShapeDtypeStruct((part, lanes), jnp.float32)] * QUARTERS
        + [jax.ShapeDtypeStruct((size, lanes), jnp.float32) for size in extra],
        in_specs=[pl.BlockSpec(memory_space=pltpu.SMEM)] + [anywhere] * (len(inputs) + len(olds)),
        out_specs=[anywhere] * (1 + QUARTERS + len(extra)),
        input_output_aliases={1 + len(inputs): 0} if olds else {},
        scratch_shapes=[
            buffer,
            buffer,
            pltpu.VMEM((wide, lanes), jnp.float32),
            pltpu.VMEM((6, points, lanes), jnp.float32),
            pltpu.SemaphoreType.DMA((4,)) if olds else pltpu.SemaphoreType.DMA,
            pltpu.SemaphoreType.DMA((QUARTERS,)),
            pltpu.SemaphoreType.DMA((2 * QUARTERS,)),
        ],
        compiler_params=pltpu.CompilerParams(vmem_limit_bytes=limit),
        cost_estimate=pl.CostEstimate(
            flops=25 * STEPS * tall * points * lanes, bytes_accessed=12 * tall * points * lanes,
            transcendentals=0,
        ),
        name=name,
    )(facts, *inputs, *olds)


def inner_steps(facts, start):
    rows, points, lanes = start.shape
    part = (rows - 2 * STEPS) // QUARTERS * points + META
    inputs = [start.reshape(-1, lanes)]
    return step_call(
        inner_kernel, "inner_steps", facts, inputs, [], rows, points, rows, QUARTERS * part, part,
        [STEPS * points, STEPS * points, 4 * STEPS * points], INNER_LIMIT,
    )


def outer_steps(facts, rows, points, ends, before, after, stepped):
    inputs = [ends, before, after]
    return step_call(
        outer_kernel, "outer_steps", facts, inputs, [stepped], rows, points, 6 * STEPS,
        2 * QUARTERS * points, 2 * points, [], OUTER_LIMIT,
    )


def combine_kernel(grids, edge, table_ref, *refs):
    inner, outer = refs[:QUARTERS], refs[QUARTERS:-2] if edge else []
    outs = refs[-2:] if edge else refs[QUARTERS : QUARTERS + 2]
    half = inner[0].shape[0] // 2 // SUB * SUB
    lanes = inner[0].shape[1]
    mine = jnp.bitwise_and(shifted_place(), 1)
    total = None
    for index in range(QUARTERS):
        head = inner[index]
        triple = jnp.max(head[2 * half : 2 * half + 1, :]).astype(jnp.int32)
        scale = jnp.max(head[2 * half + 1 : 2 * half + 2, :]) / grids
        columns = []
        for member in (1 - mine, mine):
            begin = pl.multiple_of(member * half, SUB)
            if edge:
                columns.append(head[pl.ds(begin + 2 * SUB, SUB), :])
                columns.append(outer[index][pl.ds(pl.multiple_of(member * SUB, SUB), SUB), :])
            else:
                columns.append(head[pl.ds(begin, SUB), :])
                columns.append(head[pl.ds(begin + SUB, SUB), :])
        wide = jnp.concatenate(columns, axis=1) * scale
        stack = jnp.concatenate(split_three(wide), axis=0)
        if edge:
            matrix = table_ref[index]
        else:
            matrix = table_ref[jnp.clip(triple, 0, len(TRIPLES) - 1)]
            refs[-1][index] = matrix
        term = jnp.dot(matrix, stack, preferred_element_type=jnp.float32)
        total = term if total is None else total + term
    for side, out_ref in enumerate(outs):
        for row in range(2):
            begin = (2 * side + row) * lanes
            out_ref[row] = total[:, begin : begin + lanes]


def combine(table, inner, outer, grids):
    lanes = inner[0].shape[1]
    shape = jax.ShapeDtypeStruct((2, COUNT, lanes), jnp.float32)
    chosen = jax.ShapeDtypeStruct((QUARTERS, *table.shape[1:]), table.dtype)
    return pl.pallas_call(
        lambda *refs: combine_kernel(grids, bool(outer), *refs),
        out_shape=[shape, shape] + ([] if outer else [chosen]),
        compiler_params=pltpu.CompilerParams(vmem_limit_bytes=24 * 2**20),
        cost_estimate=pl.CostEstimate(
            flops=2 * QUARTERS * 3 * SUB * COUNT * 4 * lanes, bytes_accessed=2**20, transcendentals=0
        ),
        name="combine",
    )(table, *inner, *outer)


def fill_kernel(chunks, width, with_base, where_ref, matrix_ref, *refs):
    sources = refs[:chunks]
    out_ref, scratch, sems = refs[chunks + with_base :]
    square = MLEN**2
    copies = []
    for index, source in enumerate(sources):
        lanes = source.shape[2]
        parts = split_three(jnp.concatenate([source[row] for row in range(width)], axis=1))
        level = {}
        begin = 0
        for (low, high), members in GROUPS:
            block = matrix_ref[begin : begin + square * len(members), : 3 * (high - low)]
            stack = jnp.concatenate([part[low:high] for part in parts], axis=0)
            result = jnp.dot(block, stack, preferred_element_type=jnp.float32)
            for k, member in enumerate(members):
                level[member] = result[k * square : (k + 1) * square]
            begin += square * len(members)
        nodal = dict(level)
        nodal[4] = level[4] + 0.5 * nodal[0]
        nodal[2] = level[2] + 0.5 * (nodal[0] + nodal[4])
        nodal[6] = level[6] + 0.5 * nodal[4]
        for odd in (1, 3, 5):
            nodal[odd] = level[odd] + 0.5 * (nodal[odd - 1] + nodal[odd + 1])
        nodal[7] = level[7] + 0.5 * nodal[6]
        for row in range(width):
            for c in range(MLEN):
                scratch[index * width + row, c * square : (c + 1) * square, :] = nodal[c][
                    :, row * lanes : (row + 1) * lanes
                ]
        for row in range(width):
            copy = pltpu.make_async_copy(
                scratch.at[index * width + row],
                out_ref.at[where_ref[index * width + row]],
                sems.at[index * width + row],
            )
            copy.start()
            copies.append(copy)
    for copy in copies:
        copy.wait()


def fill(where, matrix, sources, rows, base):
    width, _, lanes = sources[0].shape
    chunks = len(sources)
    with_base = 0 if base is None else 1
    args = [where, matrix, *sources] + ([base] if with_base else [])
    anywhere = pl.BlockSpec(memory_space=pl.ANY)
    vector = pl.BlockSpec(memory_space=pltpu.VMEM)
    return pl.pallas_call(
        lambda *refs: fill_kernel(chunks, width, with_base, *refs),
        out_shape=jax.ShapeDtypeStruct((rows, MLEN**3, lanes), jnp.float32),
        in_specs=[pl.BlockSpec(memory_space=pltpu.SMEM)] + [vector] * (1 + chunks) + [anywhere] * with_base,
        out_specs=anywhere,
        input_output_aliases={2 + chunks: 0} if with_base else {},
        scratch_shapes=[
            pltpu.VMEM((chunks * width, MLEN**3, lanes), jnp.float32),
            pltpu.SemaphoreType.DMA((chunks * width,)),
        ],
        compiler_params=pltpu.CompilerParams(vmem_limit_bytes=24 * 2**20),
        cost_estimate=pl.CostEstimate(
            flops=6 * chunks * width * matrix.size * lanes,
            bytes_accessed=4 * chunks * width * (MLEN**3 + COUNT) * lanes,
            transcendentals=0,
        ),
        name="fill",
    )(*args)


def per_device(initial, diffusion, drift, levels, weights):
    values = initial[0]
    rows, points, _ = values.shape
    dom_size = lax.axis_size("dom")
    grid_size = lax.axis_size("grid")
    columns = grid_size // ZLEN
    place = shifted_place()

    def swap(v, bits, offset=0):
        pairs = []
        for grid in range(grid_size):
            z, y = divmod(grid, columns)
            for dom in range(dom_size):
                origin = dom % 2 + offset
                partner = (((z - origin) % ZLEN ^ bits) + origin) % ZLEN * columns + y
                pairs.append((grid * dom_size + dom, partner * dom_size + dom))
        return lax.ppermute(v, ("grid", "dom"), pairs)

    across = lambda v: lax.ppermute(v, "grid", [(i, i ^ 1) for i in range(grid_size)])

    near = [(i, i ^ 1) for i in range(dom_size)]
    far = [(i, i - 1 + 2 * (i % 2)) for i in range(1, dom_size - 1)]
    numbers = [levels[0].astype(jnp.float32), weights.astype(jnp.float32), diffusion[0], drift[0]]
    facts = jnp.concatenate(numbers)
    stepped, *inner, before, after, ends = inner_steps(facts, values)
    before = lax.ppermute(before, "dom", near)
    after = lax.ppermute(after, "dom", far)
    inner = [inner[0]] + [swap(inner[k], 2 * k) for k in ORDER]
    stepped, *outer = outer_steps(facts, rows, points, ends, before, after, stepped)
    outer = [outer[0]] + [swap(outer[k], 2 * k) for k in ORDER]
    stepped = stepped.reshape(rows, points, -1)

    table = jnp.asarray(placing_table(), jnp.bfloat16)
    sums = []
    for pieces in ([], outer):
        theirs, mine, *rest = combine(table, inner, pieces, grid_size)
        table = rest[0] if rest else None
        partial = mine + swap(theirs, 1)
        sums.append(partial + across(partial))

    ring_sign = 1 - 2 * jnp.bitwise_and(place, 1)
    matrix = jnp.asarray(fill_matrix(), jnp.bfloat16)

    def spots(source, edge):
        source = jnp.bitwise_and(source + ZLEN, ZLEN - 1)
        begin = STEPS + 3 * source
        if not edge:
            return [begin, begin + 1]
        side = jnp.bitwise_and(source, 1) * (rows - STEPS)
        return [begin + 2, side + jnp.right_shift(source, 1)]

    ups, downs = list(sums), list(sums)
    chunks = list(sums)
    where = spots(place, 0) + spots(place, 1)
    for hop in range(1, ZLEN // 2):
        for s in range(2):
            next_up = swap(downs[s], 1)
            next_down = swap(ups[s], 1, 1)
            ups[s], downs[s] = next_up, next_down
            chunks += [next_up, next_down]
            where += spots(place + hop * ring_sign, s) + spots(place - hop * ring_sign, s)
    last = [swap(downs[0], 1), swap(ups[1], 1, 1)]
    combined = fill(jnp.stack(where), matrix, chunks, rows, None)
    last, combined = lax.optimization_barrier((last, combined))
    spot = spots(place + ZLEN // 2, 0) + spots(place + ZLEN // 2, 1)
    combined = fill(jnp.stack(spot), matrix, last, rows, combined)
    return stepped[None], combined.reshape(rows, MLEN, MLEN, MLEN, -1)


def solution(mesh):
    in_specs = (
        P("grid", "dom", None, None),
        P("grid", None),
        P("grid", None),
        P("grid", None),
        P("grid"),
    )
    out_specs = (P("grid", "dom", None, None), P("dom", None, None, None, None))
    return jax.shard_map(
        per_device, mesh=mesh, in_specs=in_specs, out_specs=out_specs, check_vma=False
    )
```

```python
import itertools

import jax
import jax.numpy as jnp
import numpy as np
from jax import lax
from jax.experimental import pallas as pl
from jax.experimental.pallas import tpu as pltpu
from jax.sharding import PartitionSpec as P

STEPS = 4
MLEN = 8
FINEST = 3
LEVEL_SUM = 6
ZLEN = 8
QUARTERS = 4
FACTS = 14
ORDER = (2, 1, 3)
INNER_LIMIT = 24 * 2**20
OUTER_LIMIT = 24 * 2**20


def rank_of(coordinate):
    if coordinate % 4 == 0:
        return 1
    return 2 if coordinate % 2 == 0 else 3


def union_points():
    points = []
    for first in (0, 4, 2, 6, 1, 3, 5, 7):
        for second, third in itertools.product(range(MLEN), repeat=2):
            if rank_of(first) + rank_of(second) + rank_of(third) <= LEVEL_SUM:
                points.append((first, second, third))
    return np.array(points, np.int32)


POINTS = union_points()
COUNT = len(POINTS)
SUB = 64
META = 8
TRIPLES = ((1, 2), (1, 3), (2, 1), (2, 2), (2, 3), (3, 1), (3, 2))
GROUPS = (((0, 48), (0,)), ((48, 96), (4,)), ((96, 160), (2, 6)), ((160, 208), (1, 3, 5, 7)))


def nodal_matrix(length_dim):
    matrix = np.eye(length_dim)
    stride = length_dim // 2
    while stride >= 1:
        for position in range(stride, length_dim, 2 * stride):
            matrix[position] = matrix[position] + 0.5 * matrix[position - stride]
            if position + stride < length_dim:
                matrix[position] = matrix[position] + 0.5 * matrix[position + stride]
        stride = stride // 2
    return matrix


def fill_matrix():
    nodal = nodal_matrix(MLEN)
    square = MLEN**2
    matrix = np.zeros((MLEN, MLEN, MLEN, COUNT))
    for column, (first, second, third) in enumerate(POINTS):
        matrix[first, :, :, column] = np.outer(nodal[:, second], nodal[:, third])
    matrix = matrix.reshape(MLEN, square, COUNT)
    packed = np.zeros((MLEN * square, 256))
    begin = 0
    for (low, high), members in GROUPS:
        block = matrix[list(members), :, low:high].reshape(-1, high - low)
        packed[begin : begin + len(block), : 3 * (high - low)] = np.tile(block, (1, 3))
        begin += len(block)
    return packed

def placing_table():
    tables = []
    for first, second in TRIPLES:
        level = (first, second, LEVEL_SUM - first - second)
        length = [2**v for v in level]
        surplus = np.ones((1, 1))
        for n in length:
            surplus = np.kron(surplus, np.round(2.0 * np.linalg.inv(nodal_matrix(n))) / 2.0)
        target = np.zeros((COUNT, SUB))
        for column, coords in enumerate(itertools.product(*[range(n) for n in length])):
            point = [c * (MLEN // n) for c, n in zip(coords, length)]
            target[np.all(POINTS == point, axis=1), column] = 1.0
        tables.append(np.tile(target @ surplus, (1, 3)))
    return np.stack(tables)


def split_three(values):
    high = values.astype(jnp.bfloat16)
    rest = values - high.astype(jnp.float32)
    middle = rest.astype(jnp.bfloat16)
    low = (rest - middle.astype(jnp.float32)).astype(jnp.bfloat16)
    return high, middle, low


class Stencil:
    def __init__(self, points, facts_ref, coef_ref):
        self.points, self.coef_ref = points, coef_ref
        levels = [facts_ref[dim].astype(jnp.int32) for dim in range(3)]
        spread = [facts_ref[4 + dim] for dim in range(5)]
        drift = [0.5 * facts_ref[9 + dim] for dim in range(5)]
        place = lax.broadcasted_iota(jnp.int32, (points, 128), 0)
        lane = lax.broadcasted_iota(jnp.int32, (8, 128), 1)
        sublane = lax.broadcasted_iota(jnp.int32, (META, 128), 0)
        offsets = [levels[1] + levels[2], levels[2], jnp.int32(0)]
        self.strides = []
        self.centre_rate = 1.0 - 2.0 * spread[0] - 2.0 * spread[4]
        for dim in range(3):
            length = jnp.left_shift(jnp.int32(1), levels[dim])
            coord = jnp.bitwise_and(jnp.right_shift(place, offsets[dim]), length - 1)
            rise, fall = spread[dim + 1] + drift[dim + 1], spread[dim + 1] - drift[dim + 1]
            coef_ref[2 * dim] = jnp.where(coord < length - 1, rise, 0.0)
            coef_ref[2 * dim + 1] = jnp.where(coord > 0, fall, 0.0)
            self.strides.append(jnp.left_shift(jnp.int32(1), offsets[dim]))
            self.centre_rate = self.centre_rate - 2.0 * spread[dim + 1]
        self.row_up, self.row_down = spread[0] + drift[0], spread[0] - drift[0]
        self.lane_up = jnp.where(lane < 127, spread[4] + drift[4], 0.0)
        self.lane_down = jnp.where(lane > 0, spread[4] - drift[4], 0.0)
        triple = (3 * levels[0] + levels[1] - 5).astype(jnp.float32)
        self.head = jnp.where(sublane == 0, triple, facts_ref[3])

    def advance(self, source, target, spans, locate, mask):
        points = self.points

        def tile(tile_index, carry):
            base = pl.multiple_of(tile_index * 8, 8)
            coefs = [self.coef_ref[i, pl.ds(base, 8), :] for i in range(6)]

            def at(row):
                return source[pl.ds(pl.multiple_of(row * points + base, 8), 8), :]

            for low, high in spans:
                below, centre = at(low - 1), at(low)
                for row in range(low, high):
                    above = at(row + 1)
                    offset = row * points + base
                    total = centre * self.centre_rate + above * self.row_up + below * self.row_down
                    total = total + pltpu.roll(centre, 127, 1) * self.lane_up
                    total = total + pltpu.roll(centre, 1, 1) * self.lane_down
                    for dim in range(3):
                        stride = self.strides[dim]
                        total = total + source[pl.ds(offset + stride, 8), :] * coefs[2 * dim]
                        total = total + source[pl.ds(offset - stride, 8), :] * coefs[2 * dim + 1]
                    total = mask(row, total)
                    target[pl.ds(pl.multiple_of(locate(row) + base, 8), 8), :] = total
                    below, centre = centre, above
            return carry

        lax.fori_loop(0, points // 8, tile, 0, unroll=4)


def shifted_place():
    columns = lax.axis_size("grid") // ZLEN
    core = jnp.bitwise_and(lax.axis_index("dom"), 1)
    return jnp.bitwise_and(lax.axis_index("grid") // columns - core + ZLEN, ZLEN - 1)


def inner_kernel(rows, points, facts_ref, start_ref, stepped_ref, *rest):
    parts, edges = rest[:QUARTERS], rest[QUARTERS : QUARTERS + 3]
    first, second, final, coef_ref, load_sem, part_sem, store_sem, third = rest[QUARTERS + 3 :]
    share = (rows - 2 * STEPS) // QUARTERS
    size = share * points
    block = size + META
    load = pltpu.make_async_copy(start_ref, first, load_sem)
    load.start()
    quarter = jnp.right_shift(shifted_place(), 1)
    stencil = Stencil(points, facts_ref, coef_ref)
    for index in range(QUARTERS):
        final[index * block + size : (index + 1) * block, :] = stencil.head
    load.wait()
    odd = jnp.bitwise_and(lax.axis_index("dom"), 1)
    halo, near, last = STEPS * points, 2 * STEPS * points, (rows - STEPS) * points
    spans = [
        (pl.multiple_of((1 - odd) * last, 8), halo, edges[0]),
        (pl.multiple_of(odd * last, 8), halo, edges[1]),
        (0, near, edges[2].at[pl.ds(0, near)]),
        (rows * points - near, near, edges[2].at[pl.ds(near, near)]),
    ]
    passed = [
        pltpu.make_async_copy(first.at[pl.ds(begin, size)], target, store_sem.at[QUARTERS + i])
        for i, (begin, size, target) in enumerate(spans)
    ]
    for copy in passed:
        copy.start()

    def located(row):
        group, inner = divmod(row - STEPS, share)
        return group * block + inner * points

    same = lambda row: row * points
    keep = lambda row, value: value
    buffers = [first, second, third, second, final]
    for step in range(1, STEPS + 1):
        place = located if step == STEPS else same
        stencil.advance(buffers[step - 1], buffers[step], [(step, rows - step)], place, keep)

    copies = []
    for index, part in enumerate(parts):
        begin = pl.multiple_of(jnp.bitwise_xor(quarter, index) * block, 8)
        copies.append(
            pltpu.make_async_copy(final.at[pl.ds(begin, block)], part, part_sem.at[index])
        )
    for index in range(QUARTERS):
        copies.append(
            pltpu.make_async_copy(
                final.at[pl.ds(index * block, size)],
                stepped_ref.at[pl.ds(STEPS * points + index * size, size)],
                store_sem.at[index],
            )
        )
    for copy in copies:
        copy.start()
    for copy in passed + copies:
        copy.wait()


def outer_kernel(rows, points, facts_ref, ends_ref, before_ref, after_ref, _, stepped_ref, *rest):
    parts = rest[:QUARTERS]
    first, second, final, coef_ref, load_sem, part_sem, store_sem = rest[QUARTERS:]
    halo, near = STEPS * points, 2 * STEPS * points
    dom = lax.axis_index("dom")
    near_side = pl.multiple_of((1 - jnp.bitwise_and(dom, 1)) * (halo + 2 * near), 8)
    far_side = pl.multiple_of(jnp.bitwise_and(dom, 1) * (halo + 2 * near), 8)
    sides = [
        (before_ref, near_side, halo),
        (ends_ref, halo, 2 * near),
        (after_ref, far_side, halo),
    ]
    loads = [
        pltpu.make_async_copy(source, first.at[pl.ds(begin, size)], load_sem.at[i])
        for i, (source, begin, size) in enumerate(sides)
    ]
    for load in loads:
        load.start()
    quarter = jnp.right_shift(shifted_place(), 1)
    keep_low = (dom > 0).astype(jnp.float32)
    keep_high = (dom < lax.axis_size("dom") - 1).astype(jnp.float32)
    stencil = Stencil(points, facts_ref, coef_ref)
    for load in loads:
        load.wait()

    strip = 3 * STEPS

    def mask(row, value):
        if row < STEPS:
            return value * keep_low
        if row >= 2 * strip - STEPS:
            return value * keep_high
        return value

    def located(row):
        side, inner = divmod(row, strip)
        return (2 * (inner - STEPS) + side) * points

    same = lambda row: row * points
    buffers = [first, second, first, second, final]
    for step in range(1, STEPS + 1):
        place = located if step == STEPS else same
        spans = [(step, strip - step), (strip + step, 2 * strip - step)]
        stencil.advance(buffers[step - 1], buffers[step], spans, place, mask)

    copies = []
    for index, part in enumerate(parts):
        begin = pl.multiple_of(jnp.bitwise_xor(quarter, index) * (2 * points), 8)
        copies.append(
            pltpu.make_async_copy(final.at[pl.ds(begin, 2 * points)], part, part_sem.at[index])
        )
    for index in range(2 * QUARTERS):
        row = index // 2 + index % 2 * (rows - STEPS)
        copies.append(
            pltpu.make_async_copy(
                final.at[pl.ds(index * points, points)],
                stepped_ref.at[pl.ds(row * points, points)],
                store_sem.at[index],
            )
        )
    for copy in copies:
        copy.start()
    for copy in copies:
        copy.wait()


def step_call(kernel, name, facts, inputs, olds, rows, points, tall, wide, part, extra, limit):
    lanes = inputs[0].shape[-1]
    anywhere = pl.BlockSpec(memory_space=pl.ANY)
    buffer = pltpu.VMEM((tall * points, lanes), jnp.float32)
    return pl.pallas_call(
        lambda *refs: kernel(rows, points, *refs),
        out_shape=[jax.ShapeDtypeStruct((rows * points, lanes), jnp.float32)]
        + [jax.ShapeDtypeStruct((part, lanes), jnp.float32)] * QUARTERS
        + [jax.ShapeDtypeStruct((size, lanes), jnp.float32) for size in extra],
        in_specs=[pl.BlockSpec(memory_space=pltpu.SMEM)] + [anywhere] * (len(inputs) + len(olds)),
        out_specs=[anywhere] * (1 + QUARTERS + len(extra)),
        input_output_aliases={1 + len(inputs): 0} if olds else {},
        scratch_shapes=[
            buffer,
            buffer,
            pltpu.VMEM((wide, lanes), jnp.float32),
            pltpu.VMEM((6, points, lanes), jnp.float32),
            pltpu.SemaphoreType.DMA((4,)) if olds else pltpu.SemaphoreType.DMA,
            pltpu.SemaphoreType.DMA((QUARTERS,)),
            pltpu.SemaphoreType.DMA((2 * QUARTERS,)),
        ]
        + ([] if olds else [buffer]),
        compiler_params=pltpu.CompilerParams(vmem_limit_bytes=limit),
        cost_estimate=pl.CostEstimate(
            flops=25 * STEPS * tall * points * lanes, bytes_accessed=12 * tall * points * lanes,
            transcendentals=0,
        ),
        name=name,
    )(facts, *inputs, *olds)


def inner_steps(facts, start):
    rows, points, lanes = start.shape
    part = (rows - 2 * STEPS) // QUARTERS * points + META
    inputs = [start.reshape(-1, lanes)]
    return step_call(
        inner_kernel, "inner_steps", facts, inputs, [], rows, points, rows, QUARTERS * part, part,
        [STEPS * points, STEPS * points, 4 * STEPS * points], INNER_LIMIT,
    )


def outer_steps(facts, rows, points, ends, before, after, stepped):
    inputs = [ends, before, after]
    return step_call(
        outer_kernel, "outer_steps", facts, inputs, [stepped], rows, points, 6 * STEPS,
        2 * QUARTERS * points, 2 * points, [], OUTER_LIMIT,
    )


def combine_kernel(grids, edge, table_ref, *refs):
    inner, outer = refs[:QUARTERS], refs[QUARTERS:-2] if edge else []
    outs = refs[-2:] if edge else refs[QUARTERS : QUARTERS + 2]
    half = inner[0].shape[0] // 2 // SUB * SUB
    lanes = inner[0].shape[1]
    mine = jnp.bitwise_and(shifted_place(), 1)
    total = None
    for index in range(QUARTERS):
        head = inner[index]
        triple = jnp.max(head[2 * half : 2 * half + 1, :]).astype(jnp.int32)
        scale = jnp.max(head[2 * half + 1 : 2 * half + 2, :]) / grids
        columns = []
        for member in (1 - mine, mine):
            begin = pl.multiple_of(member * half, SUB)
            if edge:
                columns.append(head[pl.ds(begin + 2 * SUB, SUB), :])
                columns.append(outer[index][pl.ds(pl.multiple_of(member * SUB, SUB), SUB), :])
            else:
                columns.append(head[pl.ds(begin, SUB), :])
                columns.append(head[pl.ds(begin + SUB, SUB), :])
        wide = jnp.concatenate(columns, axis=1) * scale
        stack = jnp.concatenate(split_three(wide), axis=0)
        if edge:
            matrix = table_ref[index]
        else:
            matrix = table_ref[jnp.clip(triple, 0, len(TRIPLES) - 1)]
            refs[-1][index] = matrix
        term = jnp.dot(matrix, stack, preferred_element_type=jnp.float32)
        total = term if total is None else total + term
    for side, out_ref in enumerate(outs):
        for row in range(2):
            begin = (2 * side + row) * lanes
            out_ref[row] = total[:, begin : begin + lanes]


def combine(table, inner, outer, grids):
    lanes = inner[0].shape[1]
    shape = jax.ShapeDtypeStruct((2, COUNT, lanes), jnp.float32)
    chosen = jax.ShapeDtypeStruct((QUARTERS, *table.shape[1:]), table.dtype)
    return pl.pallas_call(
        lambda *refs: combine_kernel(grids, bool(outer), *refs),
        out_shape=[shape, shape] + ([] if outer else [chosen]),
        compiler_params=pltpu.CompilerParams(vmem_limit_bytes=24 * 2**20),
        cost_estimate=pl.CostEstimate(
            flops=2 * QUARTERS * 3 * SUB * COUNT * 4 * lanes, bytes_accessed=2**20, transcendentals=0
        ),
        name="combine",
    )(table, *inner, *outer)


def fill_kernel(chunks, width, with_base, where_ref, matrix_ref, *refs):
    sources = refs[:chunks]
    out_ref, scratch, sems = refs[chunks + with_base :]
    square = MLEN**2
    copies = []
    for index, source in enumerate(sources):
        lanes = source.shape[2]
        parts = split_three(jnp.concatenate([source[row] for row in range(width)], axis=1))
        level = {}
        begin = 0
        for (low, high), members in GROUPS:
            block = matrix_ref[begin : begin + square * len(members), : 3 * (high - low)]
            stack = jnp.concatenate([part[low:high] for part in parts], axis=0)
            result = jnp.dot(block, stack, preferred_element_type=jnp.float32)
            for k, member in enumerate(members):
                level[member] = result[k * square : (k + 1) * square]
            begin += square * len(members)
        nodal = dict(level)
        nodal[4] = level[4] + 0.5 * nodal[0]
        nodal[2] = level[2] + 0.5 * (nodal[0] + nodal[4])
        nodal[6] = level[6] + 0.5 * nodal[4]
        for odd in (1, 3, 5):
            nodal[odd] = level[odd] + 0.5 * (nodal[odd - 1] + nodal[odd + 1])
        nodal[7] = level[7] + 0.5 * nodal[6]
        for row in range(width):
            for c in range(MLEN):
                scratch[index * width + row, c * square : (c + 1) * square, :] = nodal[c][
                    :, row * lanes : (row + 1) * lanes
                ]
        for row in range(width):
            copy = pltpu.make_async_copy(
                scratch.at[index * width + row],
                out_ref.at[where_ref[index * width + row]],
                sems.at[index * width + row],
            )
            copy.start()
            copies.append(copy)
    for copy in copies:
        copy.wait()


def fill(where, matrix, sources, rows, base):
    width, _, lanes = sources[0].shape
    chunks = len(sources)
    with_base = 0 if base is None else 1
    args = [where, matrix, *sources] + ([base] if with_base else [])
    anywhere = pl.BlockSpec(memory_space=pl.ANY)
    vector = pl.BlockSpec(memory_space=pltpu.VMEM)
    return pl.pallas_call(
        lambda *refs: fill_kernel(chunks, width, with_base, *refs),
        out_shape=jax.ShapeDtypeStruct((rows, MLEN**3, lanes), jnp.float32),
        in_specs=[pl.BlockSpec(memory_space=pltpu.SMEM)] + [vector] * (1 + chunks) + [anywhere] * with_base,
        out_specs=anywhere,
        input_output_aliases={2 + chunks: 0} if with_base else {},
        scratch_shapes=[
            pltpu.VMEM((chunks * width, MLEN**3, lanes), jnp.float32),
            pltpu.SemaphoreType.DMA((chunks * width,)),
        ],
        compiler_params=pltpu.CompilerParams(vmem_limit_bytes=24 * 2**20),
        cost_estimate=pl.CostEstimate(
            flops=6 * chunks * width * matrix.size * lanes,
            bytes_accessed=4 * chunks * width * (MLEN**3 + COUNT) * lanes,
            transcendentals=0,
        ),
        name="fill",
    )(*args)


def per_device(initial, diffusion, drift, levels, weights):
    values = initial[0]
    rows, points, _ = values.shape
    dom_size = lax.axis_size("dom")
    grid_size = lax.axis_size("grid")
    columns = grid_size // ZLEN
    place = shifted_place()

    def swap(v, bits, offset=0):
        pairs = []
        for grid in range(grid_size):
            z, y = divmod(grid, columns)
            for dom in range(dom_size):
                origin = dom % 2 + offset
                partner = (((z - origin) % ZLEN ^ bits) + origin) % ZLEN * columns + y
                pairs.append((grid * dom_size + dom, partner * dom_size + dom))
        return lax.ppermute(v, ("grid", "dom"), pairs)

    across = lambda v: lax.ppermute(v, "grid", [(i, i ^ 1) for i in range(grid_size)])

    near = [(i, i ^ 1) for i in range(dom_size)]
    far = [(i, i - 1 + 2 * (i % 2)) for i in range(1, dom_size - 1)]
    numbers = [levels[0].astype(jnp.float32), weights.astype(jnp.float32), diffusion[0], drift[0]]
    facts = sum(
        jnp.pad(v, (begin, FACTS - begin - v.shape[0])) for v, begin in zip(numbers, (0, 3, 4, 9))
    )
    stepped, *inner, before, after, ends = inner_steps(facts, values)
    before = lax.ppermute(before, "dom", near)
    after = lax.ppermute(after, "dom", far)
    inner = [inner[0]] + [swap(inner[k], 2 * k) for k in ORDER]
    stepped, *outer = outer_steps(facts, rows, points, ends, before, after, stepped)
    outer = [outer[0]] + [swap(outer[k], 2 * k) for k in ORDER]
    stepped = stepped.reshape(rows, points, -1)

    table = jnp.asarray(placing_table(), jnp.bfloat16)
    sums = []
    for pieces in ([], outer):
        theirs, mine, *rest = combine(table, inner, pieces, grid_size)
        table = rest[0] if rest else None
        partial = mine + swap(theirs, 1)
        sums.append(partial + across(partial))

    ring_sign = 1 - 2 * jnp.bitwise_and(place, 1)
    matrix = jnp.asarray(fill_matrix(), jnp.bfloat16)

    def spots(source, edge):
        source = jnp.bitwise_and(source + ZLEN, ZLEN - 1)
        begin = STEPS + 3 * source
        if not edge:
            return [begin, begin + 1]
        side = jnp.bitwise_and(source, 1) * (rows - STEPS)
        return [begin + 2, side + jnp.right_shift(source, 1)]

    ups, downs = list(sums), list(sums)
    chunks = list(sums)
    where = spots(place, 0) + spots(place, 1)
    for hop in range(1, ZLEN // 2):
        for s in range(2):
            next_up = swap(downs[s], 1)
            next_down = swap(ups[s], 1, 1)
            ups[s], downs[s] = next_up, next_down
            chunks += [next_up, next_down]
            where += spots(place + hop * ring_sign, s) + spots(place - hop * ring_sign, s)
    last = [swap(downs[0], 1), swap(ups[1], 1, 1)]
    combined = fill(jnp.stack(where), matrix, chunks, rows, None)
    last, combined = lax.optimization_barrier((last, combined))
    spot = spots(place + ZLEN // 2, 0) + spots(place + ZLEN // 2, 1)
    combined = fill(jnp.stack(spot), matrix, last, rows, combined)
    return stepped[None], combined.reshape(rows, MLEN, MLEN, MLEN, -1)


def solution(mesh):
    in_specs = (
        P("grid", "dom", None, None),
        P("grid", None),
        P("grid", None),
        P("grid", None),
        P("grid"),
    )
    out_specs = (P("grid", "dom", None, None), P("dom", None, None, None, None))
    return jax.shard_map(
        per_device, mesh=mesh, in_specs=in_specs, out_specs=out_specs, check_vma=False
    )
```
